128 devices in a mesh: uv: 16 (over x, y), chan: 8 (over z, core).
Axes of the slice: x: 4, y: 4, z: 4, core: 2. Of those that a mesh axis runs over, the one named last changes fastest.
Arguments:
- vis: bfloat16 [196608, 2, 1024], P('uv', None, 'chan'), may hold values from -6 to 6
- row_cell: int32 [196608], P('uv'), may hold values from 0 to 127
- tap_weight: bfloat16 [8, 196608], P(None, 'uv'), may hold values from 0.029907227 to 0.29882812
- tap_offset: int32 [8], replicated, may hold values from -32 to 32
- block_tile: int32 [1536], P('uv'), may hold values from 0 to 159, as said below
- tile_owner: int32 [160], replicated, may hold values from 0 to 15, as said below
- galaxy: bfloat16 [304, 128, 2048], P('uv', 'chan'), may hold values from -6 to 6
Outputs:
- delay_cube: bfloat16 [304, 128, 2048], P('uv', 'chan')
- cross_power: float32 [304, 1024], P('uv')
The draws below stay inside these ranges and needn't reach their ends.
Inputs may be any that keep to these rules, and one draw needn't show every extreme that they name: `tile_owner`: each of the 16 owners holds 1 to 19 tiles, and some owner exactly 19. `block_tile`: of the 96 row blocks of one index of uv, at most 11 lie in tiles of one owner, and exactly 11 lie in the tiles of some owner.
All inputs are finite; a program needn't handle non-finite values.
Results may differ from the reference program's by a relative error of at most 0.0059.
Values may be sent and summed in bfloat16 or wider, within the bound.
A program may use at most 128 MiB of HBM per device.

```python
import math
import jax
import jax.numpy as jnp
from jax import lax

CH = 1024
BR = 128
TC = 128
KT = 8
NB_DEV = 96
TILES_DEV = 10
ROWS = 196608
NTILES = 160
MAXT = 19
SLOTS = 304
N_UV = 16


def ownership(key):
    base = jax.random.fold_in(key, 7)
    key_perm, key_delta, key_shuffle = jax.random.split(base, 3)
    half = N_UV // 2
    mean_load = NB_DEV // N_UV
    owners = jax.random.permutation(key_perm, N_UV).astype(jnp.int32)
    delta = jax.random.randint(key_delta, (half,), 0, TILES_DEV).astype(jnp.int32)
    delta = delta.at[0].set(TILES_DEV - 1)
    extra = delta * mean_load // TILES_DEV
    counts_perm = jnp.concatenate([TILES_DEV + delta, TILES_DEV - delta])
    quota_perm = jnp.concatenate([mean_load + extra, mean_load - extra])
    counts = jnp.zeros((N_UV,), jnp.int32).at[owners].set(counts_perm)
    quota = jnp.zeros((N_UV,), jnp.int32).at[owners].set(quota_perm)
    owner_seq = jnp.repeat(jnp.arange(N_UV, dtype=jnp.int32), counts, total_repeat_length=NTILES)
    tile_owner = jax.random.permutation(key_shuffle, owner_seq).astype(jnp.int32)
    return (tile_owner, counts, quota)


def draw_tile_owner(key, part):
    return ownership(key)[0]


def draw_block_tile(key, part):
    tile_owner, counts, quota = ownership(key)
    by_owner = jnp.argsort(tile_owner, stable=True).astype(jnp.int32)
    start = (jnp.cumsum(counts) - counts).astype(jnp.int32)

    def one_source(source_key):
        key_order, key_pick = jax.random.split(source_key)
        seq = jnp.repeat(jnp.arange(N_UV, dtype=jnp.int32), quota, total_repeat_length=NB_DEV)
        seq = jax.random.permutation(key_order, seq)
        pick = jax.random.randint(key_pick, (NB_DEV,), 0, counts[seq]).astype(jnp.int32)
        return by_owner[start[seq] + pick]
    keys = jax.random.split(jax.random.fold_in(key, 11), N_UV)
    return jax.vmap(one_source)(keys).reshape(-1).astype(jnp.int32)


def draw_vis(key, part):
    key_vals = jax.random.fold_in(jax.random.fold_in(key, 3), 0)
    channel = jnp.arange(CH, dtype=jnp.int32)
    edge = CH // 8
    inner = (channel >= edge) & (channel < CH - edge)
    factor = jnp.where(inner, jnp.float32(0.05), jnp.float32(1.0)).astype(jnp.float32)
    values = jnp.clip(jax.random.normal(key_vals, (ROWS, 2, CH), jnp.float32), -6.0, 6.0)
    return (values * factor[None, None, :]).astype(jnp.bfloat16)


def set_ends(array, rng, low, largest):
    shape = array.shape
    index_at = [jax.random.randint(jax.random.fold_in(rng, axis), (), 0, shape[axis]) for axis in range(len(shape))]
    array = array.at[tuple(index_at)].set(low)
    longest = shape.index(max(shape))
    index_at[longest] = (index_at[longest] + 1) % shape[longest]
    return array.at[tuple(index_at)].set(largest)


def block_scale(own_key, shape, cuts, least, largest):
    level = 1.0
    for dim, blocks in cuts:
        draws = jax.random.uniform(jax.random.fold_in(jax.random.fold_in(own_key, 6), dim), (blocks,), jnp.float32, least / len(cuts), largest / len(cuts))
        level = level * jnp.repeat(jnp.exp(draws), shape[dim] // blocks).reshape((-1,) + (1,) * (len(shape) - 1 - dim))
    return level


def normal_values(stream_key, dims, spread, reach, pieces=(), held_as=jnp.bfloat16):
    factor_of = block_scale(stream_key, dims, pieces, -0.22, 0.18) if pieces else 1.0
    values = jax.random.normal(stream_key, dims, jnp.float32) * spread * factor_of
    return jnp.minimum(jnp.maximum(values, -reach), reach).astype(held_as)


def setup_inputs(seed: int = 0) -> dict:
    key_of = jax.random.split(jax.random.key(seed), 8)
    return {
        "vis": draw_vis(jax.random.fold_in(key_of[7], 71), 0),
        "row_cell": set_ends(jax.random.randint(key_of[1], (ROWS,), 0, TC), jax.random.fold_in(key_of[1], 1), 0, TC - 1).astype(jnp.int32),
        "tap_weight": jnp.clip(jnp.exp(math.log(0.29882812) - 2.30176843 * jax.random.uniform(key_of[2], (KT, ROWS), jnp.float32) ** block_scale(key_of[2], (KT, ROWS), ((1, 16),), -0.2, 0.2)), 0.029907227, 0.29882812).astype(jnp.bfloat16),
        "tap_offset": set_ends(jax.random.randint(key_of[3], (KT,), -(TC // 4), TC // 4 + 1), jax.random.fold_in(key_of[3], 1), -(TC // 4), (TC // 4 + 1) - 1).astype(jnp.int32),
        "block_tile": draw_block_tile(jax.random.fold_in(key_of[7], 71), 0),
        "tile_owner": draw_tile_owner(jax.random.fold_in(key_of[7], 71), 0),
        "galaxy": normal_values(key_of[6], (SLOTS, TC, 2 * CH), 1.0, 6.0, ((0, 16), (1, 8))),
    }


def tile_ranks(tile_owner, owners):
    onehot = (tile_owner[:, None] == jnp.arange(owners, dtype=jnp.int32)[None, :]).astype(jnp.int32)
    before = jnp.cumsum(onehot, axis=0) - onehot
    return lax.optimization_barrier(jnp.sum(before * onehot, axis=1)).astype(jnp.int32)

def kernel_matrix(cells, weights, tap_offset):
    positions = jnp.arange(TC, dtype=jnp.int32)
    total = jnp.zeros(cells.shape[:-1] + (TC, cells.shape[-1]), jnp.float32)
    for k in range(KT):
        target = cells + tap_offset[k]
        hit = target[..., None, :] == positions[:, None]
        total = total + jnp.where(hit, weights[..., k, :].astype(jnp.float32)[..., None, :], jnp.float32(0.0))
    return total.astype(jnp.bfloat16)

def delay_table():
    freq = jnp.arange(CH, dtype=jnp.int32)
    phase = (freq[:, None] * freq[None, :] % CH).astype(jnp.float32) * jnp.float32(2.0 * math.pi / CH)
    cosine = jnp.cos(phase)
    sine = jnp.sin(phase)
    x = freq.astype(jnp.float32) * jnp.float32(2.0 * math.pi / CH)
    taper = 0.35875 - 0.48829 * jnp.cos(x) + 0.14128 * jnp.cos(2.0 * x) - 0.01168 * jnp.cos(3.0 * x)
    scale = (taper / jnp.float32(math.sqrt(CH)))[:, None]
    upper = jnp.concatenate([cosine * scale, -sine * scale], axis=1)
    lower = jnp.concatenate([sine * scale, cosine * scale], axis=1)
    return jnp.concatenate([upper, lower], axis=0).astype(jnp.bfloat16)

def reference(vis, row_cell, tap_weight, tap_offset, block_tile, tile_owner, galaxy):
    nblocks = block_tile.shape[0]
    vis_blocks = vis.reshape(nblocks, BR, 2 * CH)
    cells = row_cell.reshape(nblocks, BR)
    weights = jnp.transpose(tap_weight.reshape(KT, nblocks, BR), (1, 0, 2))

    def grid_step(grid, item):
        block_vis, block_cells, block_weights, tile = item
        matrix = kernel_matrix(block_cells, block_weights, tap_offset)
        term = jnp.dot(matrix, block_vis, preferred_element_type=jnp.float32)
        return (grid.at[tile].add(term), None)
    grid, _ = lax.scan(grid_step, jnp.zeros((NTILES, TC, 2 * CH), jnp.float32), (vis_blocks, cells, weights, block_tile))
    gridded = grid.astype(jnp.bfloat16)
    delay = jnp.dot(gridded.reshape(NTILES * TC, 2 * CH), delay_table(), preferred_element_type=jnp.float32).reshape(NTILES, TC, 2 * CH)
    slots = (tile_owner * MAXT + tile_ranks(tile_owner, N_UV)).astype(jnp.int32)
    gal = galaxy[slots].astype(jnp.float32)
    product = delay[..., :CH] * gal[..., :CH] + delay[..., CH:] * gal[..., CH:]
    power_tiles = lax.optimization_barrier(jnp.sum(product, axis=1)) / jnp.float32(math.sqrt(TC))
    cube = jnp.zeros((SLOTS, TC, 2 * CH), jnp.bfloat16).at[slots].set(delay.astype(jnp.bfloat16))
    power = jnp.zeros((SLOTS, CH), jnp.float32).at[slots].set(power_tiles)
    return (cube, power)
```

```python
import functools
import math

import jax
import jax.numpy as jnp
import numpy as np
from jax import lax
from jax.experimental import pallas as pl
from jax.experimental.pallas import tpu as pltpu
from jax.sharding import PartitionSpec as P

MESH = pl.DeviceIdType.MESH
CH = 1024
BR = 128
TC = 128
KT = 8
N_OWN = 16
CAP = 11
SLOTS = 19
SIDE = 4
F32 = jnp.float32
BF16 = jnp.bfloat16
MIB = 2**20


def table_constant(n_chan):
    freq = np.arange(CH, dtype=np.int64)
    phase = ((freq[:, None] * freq[None, :]) % CH).astype(np.float32) * np.float32(2.0 * math.pi / CH)
    cosine, sine = np.cos(phase), np.sin(phase)
    x = freq.astype(np.float32) * np.float32(2.0 * math.pi / CH)
    taper = (
        np.float32(0.35875)
        - np.float32(0.48829) * np.cos(x)
        + np.float32(0.14128) * np.cos(np.float32(2.0) * x)
        - np.float32(0.01168) * np.cos(np.float32(3.0) * x)
    )
    scale = (taper / np.float32(math.sqrt(CH)))[:, None]
    upper = np.concatenate([cosine * scale, -sine * scale], axis=1)
    lower = np.concatenate([sine * scale, cosine * scale], axis=1)
    table = np.stack([upper, lower]).reshape(2, n_chan, CH // n_chan, 2 * CH)
    return table.transpose(1, 0, 2, 3).reshape(2 * CH, 2 * CH).astype(jnp.bfloat16)


def split_constant():
    p = np.zeros((2 * BR, 2 * BR), np.float32)
    r = np.arange(BR)
    p[r, 2 * r] = 1.0
    p[BR + r, 2 * r + 1] = 1.0
    return p.astype(jnp.bfloat16)


def peer(uv, chan, dx=0, dy=0):
    x = lax.rem(uv // SIDE + dx, SIDE)
    y = lax.rem(lax.rem(uv, SIDE) + dy, SIDE)
    return (x * SIDE + y, chan)


def lists_kernel(block_tile, tile_owner, blk_ref, slot_ref, rank, count):
    def clear(o, _):
        count[o] = 0
        for i in range(CAP):
            blk_ref[o, i] = 0
            slot_ref[o, i] = SLOTS
        return 0

    lax.fori_loop(0, N_OWN, clear, 0)

    def tiles(t, _):
        o = tile_owner[t]
        rank[t] = count[o]
        count[o] = count[o] + 1
        return 0

    lax.fori_loop(0, tile_owner.shape[0], tiles, 0)
    for o in range(N_OWN):
        count[o] = 0

    def blocks(b, _):
        t = block_tile[b]
        o = tile_owner[t]
        i = count[o]
        blk_ref[o, i] = b
        slot_ref[o, i] = rank[t]
        count[o] = i + 1
        return 0

    lax.fori_loop(0, block_tile.shape[0], blocks, 0)


def block_lists(block_tile, tile_owner):
    smem = pl.BlockSpec(memory_space=pltpu.SMEM)
    table = jax.ShapeDtypeStruct((N_OWN, 128), jnp.int32)
    return pl.pallas_call(
        lists_kernel,
        out_shape=(table, table),
        in_specs=[smem, smem],
        out_specs=(smem, smem),
        scratch_shapes=[pltpu.SMEM(tile_owner.shape, jnp.int32), pltpu.SMEM((N_OWN,), jnp.int32)],
        name="block_lists",
    )(block_tile, tile_owner)


def grid_send_kernel(
    blk, slot_vm, vis, target, weight, split, rec, meta, send, send_sem, recv_sem, local_sem, msend, mrecv, mlocal
):
    uv, chan = lax.axis_index("uv"), lax.axis_index("chan")
    barrier = pltpu.get_barrier_semaphore()
    for d in range(1, SIDE):
        pl.semaphore_signal(barrier, inc=1, device_id=peer(uv, chan, dx=d), device_id_type=MESH)
        pl.semaphore_signal(barrier, inc=1, device_id=peer(uv, chan, dy=d), device_id_type=MESH)
    pl.semaphore_wait(barrier, 2 * (SIDE - 1))

    def meta_copy(h, d):
        k = h * SIDE + d
        if d == 0:
            return pltpu.make_async_copy(slot_vm, meta.at[k], mlocal.at[h])
        device = peer(uv, chan, dx=d) if h == 0 else peer(uv, chan, dy=d)
        return pltpu.make_async_remote_copy(
            slot_vm, meta.at[k], msend.at[k], mrecv.at[k], device_id=device, device_id_type=MESH
        )

    for h in range(2):
        for d in range(SIDE):
            meta_copy(h, d).start()

    cells = lax.broadcasted_iota(jnp.int32, (TC, BR), 0)

    def copy(h, dx, dy):
        q = dx * SIDE + dy
        out, src = (dy, dx) if h == 0 else (dx, dy)
        if src == 0:
            return pltpu.make_async_copy(send.at[h, q], rec.at[h, out, src], local_sem.at[h, out])
        device = peer(uv, chan, dx=dx) if h == 0 else peer(uv, chan, dy=dy)
        return pltpu.make_async_remote_copy(
            send.at[h, q],
            rec.at[h, out, src],
            send_sem.at[h, out, src],
            recv_sem.at[h, out, src],
            device_id=device,
            device_id_type=MESH,
        )

    order = sorted(((dx, dy) for dx in range(SIDE) for dy in range(SIDE)), key=lambda v: (min(v) == 0, v != (2, 2)))
    for dx, dy in order:
        q = dx * SIDE + dy
        owner, _ = peer(uv, chan, dx=dx, dy=dy)
        def one(i, _, q=q, owner=owner):
            b = blk[owner, i]
            t, w = target[b], weight[b]
            total = jnp.zeros((TC, BR), F32)
            for k in range(KT):
                total = total + jnp.where(t[k : k + 1, :] == cells, w[k : k + 1, :], 0.0)
            parts = jnp.dot(split[...], vis[b], preferred_element_type=F32).astype(BF16)
            both = jnp.concatenate([parts[:BR], parts[BR:]], axis=1)
            out = jnp.dot(total.astype(BF16), both, preferred_element_type=F32).astype(BF16)
            send[0, q, i] = out[:, :BR]
            send[1, q, i] = out[:, BR:]
            return 0

        lax.fori_loop(0, CAP, one, 0, unroll=True)
        copy(0, dx, dy).start()
        copy(1, dx, dy).start()
    for h in range(2):
        for d in range(SIDE):
            meta_copy(h, d).wait()
        for dx in range(SIDE):
            for dy in range(SIDE):
                copy(h, dx, dy).wait()


def grid_send(blk, slot, vis, target, weight):
    width = vis.shape[-1]
    any_space = pl.BlockSpec(memory_space=pl.ANY)
    vmem = pl.BlockSpec(memory_space=pltpu.VMEM)
    nb = vis.shape[0]
    return pl.pallas_call(
        grid_send_kernel,
        out_shape=(
            jax.ShapeDtypeStruct((2, SIDE, SIDE, CAP, TC, width), BF16),
            jax.ShapeDtypeStruct((2 * SIDE, N_OWN, 128), jnp.int32),
        ),
        in_specs=[pl.BlockSpec(memory_space=pltpu.SMEM), vmem, vmem, vmem, vmem, vmem],
        out_specs=(any_space, any_space),
        scratch_shapes=[
            pltpu.VMEM((2, N_OWN, CAP, TC, width), BF16),
            pltpu.SemaphoreType.DMA((2, SIDE, SIDE)),
            pltpu.SemaphoreType.DMA((2, SIDE, SIDE)),
            pltpu.SemaphoreType.DMA((2, SIDE)),
            pltpu.SemaphoreType.DMA((2 * SIDE,)),
            pltpu.SemaphoreType.DMA((2 * SIDE,)),
            pltpu.SemaphoreType.DMA((2,)),
        ],
        compiler_params=pltpu.CompilerParams(collective_id=0, has_side_effects=True, vmem_limit_bytes=48 * MIB),
        name="grid_send",
    )(blk, slot, vis, target, weight, jnp.asarray(split_constant()))


def sum_kernel(meta, rec, out, acc):
    g = pl.program_id(0)
    h, off = g // SIDE, lax.rem(g, SIDE)
    uv = lax.axis_index("uv")
    x, y = uv // SIDE, lax.rem(uv, SIDE)
    shifted_x, shifted_y = lax.rem(x + off, SIDE), lax.rem(y + off, SIDE)
    owner = jnp.where(h == 0, x * SIDE + shifted_y, shifted_x * SIDE + y)
    acc[...] = jnp.zeros_like(acc)
    for d in range(SIDE):
        for i in range(CAP):
            s = meta[h * SIDE + d, owner, i]
            acc[s] = acc[s] + rec[0, 0, d, i].astype(F32)
    out[0, 0] = acc[:SLOTS].astype(BF16)


def sum_slots(meta, rec):
    width = rec.shape[-1]
    return pl.pallas_call(
        sum_kernel,
        grid=(2 * SIDE,),
        out_shape=jax.ShapeDtypeStruct((2, SIDE, SLOTS, TC, width), BF16),
        in_specs=[
            pl.BlockSpec(memory_space=pltpu.SMEM),
            pl.BlockSpec((1, 1, SIDE, CAP, TC, width), lambda g: (g // SIDE, g % SIDE, 0, 0, 0, 0)),
        ],
        out_specs=pl.BlockSpec((1, 1, SLOTS, TC, width), lambda g: (g // SIDE, g % SIDE, 0, 0, 0)),
        scratch_shapes=[pltpu.VMEM((SLOTS + 1, TC, width), F32)],
        compiler_params=pltpu.CompilerParams(vmem_limit_bytes=24 * MIB),
        name="sum_slots",
    )(meta, rec)


def delay_kernel(
    n_chan, part, table, galaxy, cube, power,
    got, piece, flat, table_vm, mine, others,
    send_sem, recv_sem, local_sem, zsend, zrecv, zlocal, psend, precv, table_sem,
):
    uv, chan = lax.axis_index("uv"), lax.axis_index("chan")
    rows = TC // n_chan

    def z_peer(d):
        return (uv, lax.rem(chan + d, n_chan))

    load_table = pltpu.make_async_copy(table, table_vm, table_sem)
    load_table.start()
    barrier = pltpu.get_barrier_semaphore()
    for d in range(1, SIDE):
        pl.semaphore_signal(barrier, inc=1, device_id=peer(uv, chan, dx=d), device_id_type=MESH)
        pl.semaphore_signal(barrier, inc=1, device_id=peer(uv, chan, dy=d), device_id_type=MESH)
    for d in range(1, n_chan):
        pl.semaphore_signal(barrier, inc=1, device_id=z_peer(d), device_id_type=MESH)
    pl.semaphore_wait(barrier, 2 * (SIDE - 1) + n_chan - 1)

    def copy(h, d):
        if d == 0:
            return pltpu.make_async_copy(part.at[h, d], got.at[h, d], local_sem.at[h])
        device = peer(uv, chan, dy=d) if h == 0 else peer(uv, chan, dx=d)
        return pltpu.make_async_remote_copy(
            part.at[h, d], got.at[h, d], send_sem.at[h, d], recv_sem.at[h, d], device_id=device, device_id_type=MESH
        )

    for d in (2, 1, 3, 0):
        for h in range(2):
            copy(h, d).start()
    for h in range(2):
        for d in range(SIDE):
            copy(h, d).wait()

    width = got.shape[-1]

    def one_slot(s, _):
        for h in range(2):
            total = got[h, 0, s].astype(F32)
            for d in range(1, SIDE):
                total = total + got[h, d, s].astype(F32)
            piece[:, s, :, h * width : (h + 1) * width] = total.astype(BF16).reshape(n_chan, rows, width)
        return 0

    lax.fori_loop(0, SLOTS, one_slot, 0)

    def z_copy(d):
        there, _ = lax.rem(chan + d, n_chan), None
        columns = pl.ds(pl.multiple_of(chan * 2 * width, 2 * width), 2 * width)
        if d == 0:
            return pltpu.make_async_copy(piece.at[there], flat.at[:, :, columns], zlocal)
        return pltpu.make_async_remote_copy(
            piece.at[there], flat.at[:, :, columns], zsend.at[d], zrecv.at[d],
            device_id=z_peer(d), device_id_type=MESH,
        )

    for d in (*range(1, n_chan), 0):
        z_copy(d).start()
    for d in range(n_chan):
        z_copy(d).wait()
    load_table.wait()

    step = 256
    x = flat[...].reshape(SLOTS * rows, 2 * CH)
    for c in range(CH // step):
        lo = slice(c * step, (c + 1) * step)
        hi = slice(CH + c * step, CH + (c + 1) * step)
        re = jnp.dot(x, table_vm[:, lo], preferred_element_type=F32).reshape(SLOTS, rows, step)
        im = jnp.dot(x, table_vm[:, hi], preferred_element_type=F32).reshape(SLOTS, rows, step)
        cube[:, :, lo] = re.astype(BF16)
        cube[:, :, hi] = im.astype(BF16)
        product = re * galaxy[:, :, lo].astype(F32) + im * galaxy[:, :, hi].astype(F32)
        mine[:, lo] = jnp.sum(product, axis=1)

    def p_copy(d):
        return pltpu.make_async_remote_copy(
            mine, others.at[d - 1], psend.at[d - 1], precv.at[d - 1], device_id=z_peer(d), device_id_type=MESH
        )

    for d in range(1, n_chan):
        p_copy(d).start()
    for d in range(1, n_chan):
        p_copy(d).wait()
    total = mine[...]
    for d in range(n_chan - 1):
        total = total + others[d]
    power[...] = total / F32(math.sqrt(TC))


def delay_power(n_chan, part, galaxy):
    width = part.shape[-1]
    rows = TC // n_chan
    vmem = pl.BlockSpec(memory_space=pltpu.VMEM)
    any_space = pl.BlockSpec(memory_space=pl.ANY)
    dma = pltpu.SemaphoreType.DMA
    return pl.pallas_call(
        functools.partial(delay_kernel, n_chan),
        out_shape=(
            jax.ShapeDtypeStruct((SLOTS, rows, 2 * CH), BF16),
            jax.ShapeDtypeStruct((SLOTS, CH), F32),
        ),
        in_specs=[any_space, any_space, vmem],
        out_specs=(vmem, vmem),
        scratch_shapes=[
            pltpu.VMEM((2, SIDE, SLOTS, TC, width), BF16),
            pltpu.VMEM((n_chan, SLOTS, rows, 2 * width), BF16),
            pltpu.VMEM((SLOTS, rows, 2 * CH), BF16),
            pltpu.VMEM((2 * CH, 2 * CH), BF16),
            pltpu.VMEM((SLOTS, CH), F32),
            pltpu.VMEM((n_chan - 1, SLOTS, CH), F32),
            dma((2, SIDE)),
            dma((2, SIDE)),
            dma((2,)),
            dma((n_chan,)),
            dma((n_chan,)),
            dma,
            dma((n_chan - 1,)),
            dma((n_chan - 1,)),
            dma,
        ],
        compiler_params=pltpu.CompilerParams(collective_id=1, has_side_effects=True, vmem_limit_bytes=48 * MIB),
        name="delay_power",
    )(part, jnp.asarray(table_constant(n_chan)), galaxy)


def solution(mesh):
    n_chan = mesh.shape["chan"]

    def body(vis, row_cell, tap_weight, tap_offset, block_tile, tile_owner, galaxy):
        nb = block_tile.shape[0]
        blk, slot = block_lists(block_tile, tile_owner)
        blocks = vis.reshape(nb, 2 * BR, vis.shape[2])
        target = row_cell.reshape(nb, 1, BR) + tap_offset[None, :, None]
        weight = jnp.transpose(tap_weight.reshape(KT, nb, BR), (1, 0, 2)).astype(F32)
        rec, meta = grid_send(blk, slot, blocks, target, weight)
        part = sum_slots(meta, rec)
        return delay_power(n_chan, part, galaxy)

    return jax.shard_map(
        body,
        mesh=mesh,
        in_specs=(
            P("uv", None, "chan"),
            P("uv"),
            P(None, "uv"),
            P(),
            P("uv"),
            P(),
            P("uv", "chan", None),
        ),
        out_specs=(P("uv", "chan", None), P("uv", None)),
        check_vma=False,
    )
```

```python
import functools
import math

import jax
import jax.numpy as jnp
import numpy as np
from jax import lax
from jax.experimental import pallas as pl
from jax.experimental.pallas import tpu as pltpu
from jax.sharding import PartitionSpec as P

MESH = pl.DeviceIdType.MESH
CH = 1024
BR = 128
TC = 128
KT = 8
N_OWN = 16
CAP = 11
SLOTS = 19
BLOCKS = 96
TILES = 160
SIDE = 4
ORDER = (2, 1, 3, 0)
F32 = jnp.float32
BF16 = jnp.bfloat16
MIB = 2**20


def table_constant(n_chan):
    freq = np.arange(CH, dtype=np.int64)
    phase = ((freq[:, None] * freq[None, :]) % CH).astype(np.float32) * np.float32(2.0 * math.pi / CH)
    cosine, sine = np.cos(phase), np.sin(phase)
    x = freq.astype(np.float32) * np.float32(2.0 * math.pi / CH)
    taper = (
        np.float32(0.35875)
        - np.float32(0.48829) * np.cos(x)
        + np.float32(0.14128) * np.cos(np.float32(2.0) * x)
        - np.float32(0.01168) * np.cos(np.float32(3.0) * x)
    )
    scale = (taper / np.float32(math.sqrt(CH)))[:, None]
    upper = np.concatenate([cosine * scale, -sine * scale], axis=1)
    lower = np.concatenate([sine * scale, cosine * scale], axis=1)
    table = np.stack([upper, lower]).reshape(2, n_chan, CH // n_chan, 2 * CH)
    return table.transpose(1, 0, 2, 3).reshape(2 * CH, 2 * CH).astype(jnp.bfloat16)


def split_constant():
    p = np.zeros((2 * BR, 2 * BR), np.float32)
    r = np.arange(BR)
    p[r, 2 * r] = 1.0
    p[BR + r, 2 * r + 1] = 1.0
    return p.astype(jnp.bfloat16)


def peer(uv, chan, dx=0, dy=0):
    x = lax.rem(uv // SIDE + dx, SIDE)
    y = lax.rem(lax.rem(uv, SIDE) + dy, SIDE)
    return (x * SIDE + y, chan)


def column(row):
    return jnp.transpose(jnp.broadcast_to(row, (128, 128)))


def tall(row):
    return jnp.concatenate([column(row[:, :128]), column(row[:, 128:])], axis=0)


def position_in_order(d):
    return jnp.where(d == 2, 0, jnp.where(d == 1, 1, jnp.where(d == 3, 2, 3)))


def count(mask):
    return jnp.where(mask, 1, 0)


def make_tables(x, y, tb, lists, places):
    tile_r, own_r = tb[0:1, :128], tb[1:2, :]
    lane = lax.broadcasted_iota(jnp.int32, (128, 128), 1)
    sub = lax.broadcasted_iota(jnp.int32, (128, 128), 0)
    tile_c = column(tile_r)
    lane_t = lax.broadcasted_iota(jnp.int32, (256, 128), 1)
    t_c = lax.broadcasted_iota(jnp.int32, (256, 128), 0)
    own_c = tall(own_r)
    match = tile_r == t_c
    number_c = jnp.sum(count(match), axis=1, keepdims=True)
    number_r = [jnp.sum(count(tile_c == lane + 128 * i), axis=0, keepdims=True) for i in range(2)]
    same = [own_r[:, 128 * i : 128 * (i + 1)] == own_c for i in range(2)]
    rank_c = sum(jnp.sum(count(same[i] & (lane_t + 128 * i < t_c)), axis=1, keepdims=True) for i in range(2))
    earlier_r = jnp.sum(count((tile_c == tile_r) & (sub < lane)), axis=0, keepdims=True)
    repeat_c = count(column(earlier_r) > 0)
    dx_c, dy_c = ((own_c >> 2) - x) & 3, ((own_c & 3) - y) & 3
    slot_key = jnp.where(t_c < TILES, own_c * 32 + rank_c, -1)
    start_c = sum(
        jnp.sum(jnp.where(same[i] & (lane_t + 128 * i < t_c), number_r[i], 0), axis=1, keepdims=True) for i in range(2)
    )
    last_c = jnp.where(number_c > 0, start_c + number_c, 0)
    for i in range(4):
        hit = slot_key == lane_t + 128 * i
        places[i : i + 1, :] = jnp.sum(jnp.where(hit, last_c, 0), axis=0, keepdims=True) - 1
    for h in range(2):
        group_c, inner_c = (dx_c, dy_c) if h == 0 else (dy_c, dx_c)
        first_c = group_c * 64 + position_in_order(inner_c) * CAP + start_c
        key_r = jnp.sum(jnp.where(match, first_c, 0), axis=0, keepdims=True) + earlier_r
        key_c = column(jnp.where(lane[0:1] < BLOCKS, key_r, -1))
        for i in range(2):
            hit = key_c == lane + 128 * i
            row = 4 * h + i
            lists[row : row + 1, :] = jnp.sum(jnp.where(hit, sub, 0), axis=0, keepdims=True)
            lists[row + 2 : row + 3, :] = jnp.sum(jnp.where(hit, repeat_c, 0), axis=0, keepdims=True)


def kernel(
    n_chan, cuts,
    block_tile, tile_owner, tap_offset, cells, weight, split, vis_hbm, table_hbm, galaxy_hbm,
    cube, power,
    vis, table, galaxy, tb, lists, places, lists_sm, places_sm, carry, send, rec0, rec1, rec2, rec3, part, got, piece, flat,
    mine, shares, total_power,
    load_sem, msend, mrecv, sm_sem, asend, arecv, bsend, brecv, zsend, zrecv, zlocal, psend, precv, gsend, grecv,
):
    uv, chan = lax.axis_index("uv"), lax.axis_index("chan")
    x, y = uv // SIDE, lax.rem(uv, SIDE)
    rows = TC // n_chan
    width = vis.shape[-1]
    recs = (rec0, rec1, rec2, rec3)

    def z_peer(d):
        return (uv, lax.rem(chan + d, n_chan))

    def xy_peer(h, d):
        return peer(uv, chan, dx=d) if h == 0 else peer(uv, chan, dy=d)

    loads = [
        pltpu.make_async_copy(vis_hbm, vis, load_sem.at[0]),
        pltpu.make_async_copy(table_hbm, table, load_sem.at[1]),
        pltpu.make_async_copy(galaxy_hbm, galaxy, load_sem.at[2]),
    ]
    loads[0].start()
    barrier = pltpu.get_barrier_semaphore()
    for h in range(2):
        for d in range(1, SIDE):
            pl.semaphore_signal(barrier, inc=1, device_id=xy_peer(h, d), device_id_type=MESH)
    for d in range(1, n_chan):
        pl.semaphore_signal(barrier, inc=1, device_id=z_peer(d), device_id_type=MESH)

    tb[...] = jnp.full(tb.shape, -1, jnp.int32)
    tb[0:1, 0 : block_tile.shape[1]] = block_tile[...]
    tb[1:2, 0 : tile_owner.shape[1]] = tile_owner[...]
    make_tables(x, y, tb, lists, places.at[0])
    places[SIDE] = places[0]
    to_scalars = pltpu.make_async_copy(lists, lists_sm, sm_sem.at[0])
    to_scalars.start()
    pl.semaphore_wait(barrier, 2 * (SIDE - 1) + n_chan - 1)

    def places_copy(h, d):
        k = h * SIDE + d
        return pltpu.make_async_remote_copy(
            places.at[0], places.at[k], msend.at[k], mrecv.at[k], device_id=xy_peer(h, d), device_id_type=MESH
        )

    for h in range(2):
        for d in range(1, SIDE):
            if h == 0:
                places_copy(h, d).start()
    for d in range(1, SIDE):
        places_copy(1, d).start()
    carry[...] = jnp.zeros_like(carry)
    to_scalars.wait()
    loads[0].wait()
    loads[1].start()
    loads[2].start()

    def a_copy(h, g, k):
        n, size = cuts[k] // CAP, cuts[k + 1] - cuts[k]
        return pltpu.make_async_remote_copy(
            send.at[h, g - 1, pl.ds(cuts[k], size)], recs[n].at[h, g, pl.ds(cuts[k] - n * CAP, size)], asend.at[h, g - 1, k], arecv.at[h, g - 1, k],
            device_id=xy_peer(h, g), device_id_type=MESH,
        )

    cell_rows = lax.broadcasted_iota(jnp.int32, (TC, BR), 0)

    def place(n, p, _):
        for g in ORDER:
            for h in range(2):
                row, at = 4 * h + g // 2, 64 * (g % 2) + p
                b = jnp.minimum(lists_sm[row, at], BLOCKS - 1)
                keep = lists_sm[row + 2, at].astype(F32)
                away = cell_rows - cells[b]
                w = weight[b]
                matrix = jnp.zeros((TC, BR), F32)
                for k in range(KT):
                    matrix = matrix + jnp.where(away == tap_offset[k], w[k : k + 1, :], 0.0)
                half = jnp.dot(split[h], vis[b], preferred_element_type=F32).astype(BF16)
                out = jnp.dot(matrix.astype(BF16), half, preferred_element_type=F32)
                out = out + keep * carry[h, g]
                carry[h, g] = out
                if g == 0:
                    recs[n][h, 0, p - n * CAP] = out.astype(BF16)
                else:
                    send[h, g - 1, p] = out.astype(BF16)
        return 0

    n_cuts = len(cuts) - 1
    for k in range(n_cuts):
        lax.fori_loop(cuts[k], cuts[k + 1], functools.partial(place, cuts[k] // CAP), 0)
        for g in ORDER[:3]:
            for h in range(2):
                a_copy(h, g, k).start()

    for h in range(2):
        for d in range(1, SIDE):
            places_copy(h, d).wait()
    places_load = pltpu.make_async_copy(places, places_sm, sm_sem.at[1])
    places_load.start()
    places_load.wait()

    slot_cuts = (0, 10, SLOTS)

    def b_copy(h, off, q):
        cut = pl.ds(slot_cuts[q], slot_cuts[q + 1] - slot_cuts[q])
        return pltpu.make_async_remote_copy(
            part.at[h, off - 1, cut], got.at[h, off, cut], bsend.at[h, off - 1, q], brecv.at[h, off - 1, q],
            device_id=xy_peer(1 - h, off), device_id_type=MESH,
        )

    arrived = 0
    for n, off in enumerate(ORDER):
        needed = CAP * (n + 1)
        while cuts[arrived] < needed:
            for h in range(2):
                for g in range(1, SIDE):
                    a_copy(h, g, arrived).wait_recv()
            arrived += 1
        for h in range(2):
            ox = x if h == 0 else lax.rem(x + off, SIDE)
            oy = lax.rem(y + off, SIDE) if h == 0 else y

            def one(s, _, h=h, off=off, rec=recs[n], ox=ox, oy=oy):
                total = jnp.zeros((TC, width), F32)
                for d in range(SIDE):
                    p = places_sm[h * SIDE + d, ox, 32 * oy + s]
                    there = jnp.where(p >= 0, F32(1.0), F32(0.0))
                    at = jnp.clip(p, 0, CAP - 1)
                    total = total + there * rec[h, d, at].astype(F32)
                if off == 0:
                    got[h, 0, s] = total.astype(BF16)
                else:
                    part[h, off - 1, s] = total.astype(BF16)
                return 0

            lax.fori_loop(0, SLOTS, one, 0)
            if off:
                for q in range(2):
                    b_copy(h, off, q).start()

    def z_copy(d, q):
        there = lax.rem(chan + d, n_chan)
        columns = pl.ds(pl.multiple_of(chan * 2 * width, 2 * width), 2 * width)
        cut = pl.ds(slot_cuts[q], slot_cuts[q + 1] - slot_cuts[q])
        if d == 0:
            return pltpu.make_async_copy(piece.at[there, cut], flat.at[cut, :, columns], zlocal.at[q])
        return pltpu.make_async_remote_copy(
            piece.at[there, cut], flat.at[cut, :, columns], zsend.at[d - 1, q], zrecv.at[d - 1, q],
            device_id=z_peer(d), device_id_type=MESH,
        )

    def one_slot(s, _):
        for h in range(2):
            total = got[h, 0, s].astype(F32)
            for d in range(1, SIDE):
                total = total + got[h, d, s].astype(F32)
            piece[:, s, :, h * width : (h + 1) * width] = total.astype(BF16).reshape(n_chan, rows, width)
        return 0

    for q in range(2):
        for h in range(2):
            for off in range(1, SIDE):
                b_copy(h, off, q).wait_recv()
        lax.fori_loop(slot_cuts[q], slot_cuts[q + 1], one_slot, 0)
        for d in (*range(1, n_chan), 0):
            z_copy(d, q).start()
    loads[1].wait()
    loads[2].wait()

    step = 256
    for q in range(2):
        for d in range(n_chan):
            if d == 0:
                z_copy(d, q).wait()
            else:
                z_copy(d, q).wait_recv()
        lo_s, hi_s = slot_cuts[q], slot_cuts[q + 1]
        v = flat[lo_s:hi_s].reshape((hi_s - lo_s) * rows, 2 * CH)
        for c in range(CH // step):
            lo = slice(c * step, (c + 1) * step)
            hi = slice(CH + c * step, CH + (c + 1) * step)
            re = jnp.dot(v, table[:, lo], preferred_element_type=F32).reshape(hi_s - lo_s, rows, step)
            im = jnp.dot(v, table[:, hi], preferred_element_type=F32).reshape(hi_s - lo_s, rows, step)
            cube[lo_s:hi_s, :, lo] = re.astype(BF16)
            cube[lo_s:hi_s, :, hi] = im.astype(BF16)
            product = re * galaxy[lo_s:hi_s, :, lo].astype(F32) + im * galaxy[lo_s:hi_s, :, hi].astype(F32)
            mine[lo_s:hi_s, lo] = jnp.sum(product, axis=1)

    share = CH // n_chan

    def share_columns(c):
        return pl.ds(pl.multiple_of(c * share, share), share)

    def p_copy(d):
        return pltpu.make_async_remote_copy(
            mine.at[:, share_columns(lax.rem(chan + d, n_chan))], shares.at[d - 1], psend.at[d - 1], precv.at[d - 1],
            device_id=z_peer(d), device_id_type=MESH,
        )

    def g_copy(d):
        own = total_power.at[:, share_columns(chan)]
        return pltpu.make_async_remote_copy(
            own, own, gsend.at[d - 1], grecv.at[d - 1], device_id=z_peer(d), device_id_type=MESH
        )

    for d in range(1, n_chan):
        p_copy(d).start()
    total = mine[:, share_columns(chan)]
    for d in range(1, n_chan):
        p_copy(d).wait_recv()
        total = total + shares[d - 1]
    total_power[:, share_columns(chan)] = total / F32(math.sqrt(TC))
    for d in range(1, n_chan):
        g_copy(d).start()
    for h in range(2):
        for g in range(1, SIDE):
            for k in range(n_cuts):
                a_copy(h, g, k).wait_send()
            for q in range(2):
                b_copy(h, g, q).wait_send()
    for d in range(1, n_chan):
        for q in range(2):
            z_copy(d, q).wait_send()
        p_copy(d).wait_send()
    for d in range(1, n_chan):
        g_copy(d).wait()
    power[...] = total_power[...]


def fused(n_chan, cuts, block_tile, tile_owner, tap_offset, cells, weight, vis, galaxy):
    nb, _, width = vis.shape
    n_cuts = len(cuts) - 1
    rows = TC // n_chan
    smem = pl.BlockSpec(memory_space=pltpu.SMEM)
    vmem = pl.BlockSpec(memory_space=pltpu.VMEM)
    hbm = pl.BlockSpec(memory_space=pl.ANY)
    dma = pltpu.SemaphoreType.DMA
    return pl.pallas_call(
        functools.partial(kernel, n_chan, cuts),
        out_shape=(
            jax.ShapeDtypeStruct((SLOTS, rows, 2 * CH), BF16),
            jax.ShapeDtypeStruct((SLOTS, CH), F32),
        ),
        in_specs=[vmem, vmem, smem, vmem, vmem, vmem, hbm, hbm, hbm],
        out_specs=(vmem, vmem),
        scratch_shapes=[
            pltpu.VMEM(vis.shape, BF16),
            pltpu.VMEM((2 * CH, 2 * CH), BF16),
            pltpu.VMEM(galaxy.shape, BF16),
            pltpu.VMEM((8, 256), jnp.int32),
            pltpu.VMEM((8, 128), jnp.int32),
            pltpu.VMEM((2 * SIDE, 8, 128), jnp.int32),
            pltpu.SMEM((8, 128), jnp.int32),
            pltpu.SMEM((2 * SIDE, 8, 128), jnp.int32),
            pltpu.VMEM((2, SIDE, TC, width), F32),
            pltpu.VMEM((2, SIDE - 1, SIDE * CAP, TC, width), BF16),
            *[pltpu.VMEM((2, SIDE, CAP, TC, width), BF16) for _ in range(SIDE)],
            pltpu.VMEM((2, SIDE - 1, SLOTS, TC, width), BF16),
            pltpu.VMEM((2, SIDE, SLOTS, TC, width), BF16),
            pltpu.VMEM((n_chan, SLOTS, rows, 2 * width), BF16),
            pltpu.VMEM((SLOTS, rows, 2 * CH), BF16),
            pltpu.VMEM((SLOTS, CH), F32),
            pltpu.VMEM((n_chan - 1, SLOTS, CH // n_chan), F32),
            pltpu.VMEM((SLOTS, CH), F32),
            dma((3,)),
            dma((2 * SIDE,)),
            dma((2 * SIDE,)),
            dma((2,)),
            dma((2, SIDE - 1, n_cuts)),
            dma((2, SIDE - 1, n_cuts)),
            dma((2, SIDE - 1, 2)),
            dma((2, SIDE - 1, 2)),
            dma((n_chan - 1, 2)),
            dma((n_chan - 1, 2)),
            dma((2,)),
            dma((n_chan - 1,)),
            dma((n_chan - 1,)),
            dma((n_chan - 1,)),
            dma((n_chan - 1,)),
        ],
        compiler_params=pltpu.CompilerParams(collective_id=0, has_side_effects=True, vmem_limit_bytes=60 * MIB),
        name="grid_delay",
    )(
        block_tile.reshape(1, -1), tile_owner.reshape(1, -1), tap_offset, cells, weight,
        jnp.asarray(split_constant().reshape(2, BR, 2 * BR)), vis, jnp.asarray(table_constant(n_chan)), galaxy,
    )


def solution(mesh):
    n_chan = mesh.shape["chan"]

    def body(vis, row_cell, tap_weight, tap_offset, block_tile, tile_owner, galaxy):
        nb = block_tile.shape[0]
        blocks = vis.reshape(nb, 2 * BR, vis.shape[2])
        cells = row_cell.reshape(nb, 1, BR)
        weight = jnp.transpose(tap_weight.reshape(KT, nb, BR), (1, 0, 2)).astype(F32)
        return fused(
            n_chan, (0, 3, 11, 22, 33, 44), block_tile, tile_owner, tap_offset, cells, weight, blocks, galaxy
        )

    return jax.shard_map(
        body,
        mesh=mesh,
        in_specs=(
            P("uv", None, "chan"),
            P("uv"),
            P(None, "uv"),
            P(),
            P("uv"),
            P(),
            P("uv", "chan", None),
        ),
        out_specs=(P("uv", "chan", None), P("uv", None)),
        check_vma=False,
    )
```

```python
import functools
import math

import jax
import jax.numpy as jnp
import numpy as np
from jax import lax
from jax.experimental import pallas as pl
from jax.experimental.pallas import tpu as pltpu
from jax.sharding import PartitionSpec as P

MESH = pl.DeviceIdType.MESH
CH = 1024
BR = 128
TC = 128
KT = 8
N_OWN = 16
CAP = 11
SLOTS = 19
BLOCKS = 96
TILES = 160
SIDE = 4
ORDER = (2, 1, 3, 0)
F32 = jnp.float32
BF16 = jnp.bfloat16
MIB = 2**20


def table_constant(n_chan):
    freq = np.arange(CH, dtype=np.int64)
    phase = ((freq[:, None] * freq[None, :]) % CH).astype(np.float32) * np.float32(2.0 * math.pi / CH)
    cosine, sine = np.cos(phase), np.sin(phase)
    x = freq.astype(np.float32) * np.float32(2.0 * math.pi / CH)
    taper = (
        np.float32(0.35875)
        - np.float32(0.48829) * np.cos(x)
        + np.float32(0.14128) * np.cos(np.float32(2.0) * x)
        - np.float32(0.01168) * np.cos(np.float32(3.0) * x)
    )
    scale = (taper / np.float32(math.sqrt(CH)))[:, None]
    upper = np.concatenate([cosine * scale, -sine * scale], axis=1)
    lower = np.concatenate([sine * scale, cosine * scale], axis=1)
    table = np.stack([upper, lower]).reshape(2, n_chan, CH // n_chan, 2 * CH)
    return table.transpose(1, 0, 2, 3).reshape(2 * CH, 2 * CH).astype(jnp.bfloat16)


def peer(uv, chan, dx=0, dy=0):
    x = lax.rem(uv // SIDE + dx, SIDE)
    y = lax.rem(lax.rem(uv, SIDE) + dy, SIDE)
    return (x * SIDE + y, chan)


def column(row):
    return jnp.transpose(jnp.broadcast_to(row, (128, 128)))


def tall(row):
    return jnp.concatenate([column(row[:, :128]), column(row[:, 128:])], axis=0)


def position_in_order(d):
    return jnp.where(d == 2, 0, jnp.where(d == 1, 1, jnp.where(d == 3, 2, 3)))


def count(mask):
    return jnp.where(mask, 1, 0)


def make_tables(x, y, tb, lists, places):
    tile_r, own_r = tb[0:1, :128], tb[1:2, :]
    lane = lax.broadcasted_iota(jnp.int32, (128, 128), 1)
    sub = lax.broadcasted_iota(jnp.int32, (128, 128), 0)
    tile_c = column(tile_r)
    lane_t = lax.broadcasted_iota(jnp.int32, (256, 128), 1)
    t_c = lax.broadcasted_iota(jnp.int32, (256, 128), 0)
    own_c = tall(own_r)
    match = tile_r == t_c
    number_c = jnp.sum(count(match), axis=1, keepdims=True)
    number_r = [jnp.sum(count(tile_c == lane + 128 * i), axis=0, keepdims=True) for i in range(2)]
    same = [own_r[:, 128 * i : 128 * (i + 1)] == own_c for i in range(2)]
    rank_c = sum(jnp.sum(count(same[i] & (lane_t + 128 * i < t_c)), axis=1, keepdims=True) for i in range(2))
    earlier_r = jnp.sum(count((tile_c == tile_r) & (sub < lane)), axis=0, keepdims=True)
    repeat_c = count(column(earlier_r) > 0)
    dx_c, dy_c = ((own_c >> 2) - x) & 3, ((own_c & 3) - y) & 3
    slot_key = jnp.where(t_c < TILES, own_c * 32 + rank_c, -1)
    start_c = sum(
        jnp.sum(jnp.where(same[i] & (lane_t + 128 * i < t_c), number_r[i], 0), axis=1, keepdims=True) for i in range(2)
    )
    last_c = jnp.where(number_c > 0, start_c + number_c, 0)
    for i in range(4):
        hit = slot_key == lane_t + 128 * i
        places[i : i + 1, :] = jnp.sum(jnp.where(hit, last_c, 0), axis=0, keepdims=True) - 1
    for h in range(2):
        group_c, inner_c = (dx_c, dy_c) if h == 0 else (dy_c, dx_c)
        first_c = group_c * 64 + position_in_order(inner_c) * CAP + start_c
        key_r = jnp.sum(jnp.where(match, first_c, 0), axis=0, keepdims=True) + earlier_r
        key_c = column(jnp.where(lane[0:1] < BLOCKS, key_r, -1))
        for i in range(2):
            hit = key_c == lane + 128 * i
            row = 4 * h + i
            lists[row : row + 1, :] = jnp.sum(jnp.where(hit, sub, 0), axis=0, keepdims=True)
            lists[row + 2 : row + 3, :] = jnp.sum(jnp.where(hit, repeat_c, 0), axis=0, keepdims=True)


def kernel(
    n_chan, cuts,
    block_tile, tile_owner, tap_offset, cells, weight, vis_hbm, table_hbm, galaxy_hbm,
    cube, power,
    vis, wide, table, galaxy, tb, lists, places, lists_sm, places_sm, carry, send, rec0, rec1, rec2, rec3, part, via, got, piece, flat,
    mine, shares, total_power,
    load_sem, msend, mrecv, sm_sem, asend, arecv, bsend, brecv, vsend, vrecv, zsend, zrecv, zlocal, psend, precv, gsend, grecv,
):
    uv, chan = lax.axis_index("uv"), lax.axis_index("chan")
    x, y = uv // SIDE, lax.rem(uv, SIDE)
    rows = TC // n_chan
    width = vis.shape[-1]
    recs = (rec0, rec1, rec2, rec3)

    def z_peer(d):
        return (uv, lax.rem(chan + d, n_chan))

    def xy_peer(h, d):
        return peer(uv, chan, dx=d) if h == 0 else peer(uv, chan, dy=d)

    loads = [
        pltpu.make_async_copy(table_hbm, table, load_sem.at[0]),
        pltpu.make_async_copy(galaxy_hbm, galaxy, load_sem.at[1]),
    ]
    quarter = BLOCKS // 4
    vis_loads = [
        pltpu.make_async_copy(
            vis_hbm.at[pl.ds(i * quarter, quarter)], vis.at[pl.ds(i * quarter, quarter)], load_sem.at[2 + i]
        )
        for i in range(4)
    ]
    for load in vis_loads:
        load.start()
    barrier = pltpu.get_barrier_semaphore()
    for h in range(2):
        for d in range(1, SIDE):
            pl.semaphore_signal(barrier, inc=1, device_id=xy_peer(h, d), device_id_type=MESH)
    for d in range(1, n_chan):
        pl.semaphore_signal(barrier, inc=1, device_id=z_peer(d), device_id_type=MESH)

    tb[...] = jnp.full(tb.shape, -1, jnp.int32)
    tb[0:1, 0 : block_tile.shape[1]] = block_tile[...]
    tb[1:2, 0 : tile_owner.shape[1]] = tile_owner[...]
    make_tables(x, y, tb, lists, places.at[0])
    places[SIDE] = places[0]
    to_scalars = pltpu.make_async_copy(lists, lists_sm, sm_sem.at[0])
    to_scalars.start()

    def split(i, _):
        for j in range(4):
            b = 4 * i + j
            wide[2 * BR * j : 2 * BR * (j + 1), :] = vis[b].astype(F32)
            for part_of in range(2):
                rows_of = wide[pl.ds(2 * BR * j + part_of, BR, stride=2), :]
                vis[b, BR * part_of : BR * (part_of + 1), :] = rows_of.astype(BF16)
        return 0

    for i, load in enumerate(vis_loads):
        load.wait()
        lax.fori_loop(i * quarter // 4, (i + 1) * quarter // 4, split, 0)
    pl.semaphore_wait(barrier, 2 * (SIDE - 1) + n_chan - 1)

    def places_copy(h, d):
        k = h * SIDE + d
        return pltpu.make_async_remote_copy(
            places.at[0], places.at[k], msend.at[k], mrecv.at[k], device_id=xy_peer(h, d), device_id_type=MESH
        )

    for h in range(2):
        for d in range(1, SIDE):
            if h == 0:
                places_copy(h, d).start()
    for d in range(1, SIDE):
        places_copy(1, d).start()
    carry[...] = jnp.zeros_like(carry)
    to_scalars.wait()
    loads[0].start()
    loads[1].start()

    def a_copy(h, g, k):
        n, size = cuts[k] // CAP, cuts[k + 1] - cuts[k]
        return pltpu.make_async_remote_copy(
            send.at[h, g - 1, pl.ds(cuts[k], size)], recs[n].at[h, g, pl.ds(cuts[k] - n * CAP, size)], asend.at[h, g - 1, k], arecv.at[h, g - 1, k],
            device_id=xy_peer(h, g), device_id_type=MESH,
        )

    cell_rows = lax.broadcasted_iota(jnp.int32, (TC, BR), 0)

    def place(n, p, _):
        for g in ORDER:
            for h in range(2):
                row, at = 4 * h + g // 2, 64 * (g % 2) + p
                b = jnp.minimum(lists_sm[row, at], BLOCKS - 1)
                keep = lists_sm[row + 2, at].astype(F32)
                away = cell_rows - cells[b]
                w = weight[b]
                matrix = jnp.zeros((TC, BR), F32)
                for k in range(KT):
                    matrix = matrix + jnp.where(away == tap_offset[k], w[k : k + 1, :], 0.0)
                half = vis[b, BR * h : BR * (h + 1), :]
                out = jnp.dot(matrix.astype(BF16), half, preferred_element_type=F32)
                out = out + keep * carry[h, g]
                carry[h, g] = out
                if g == 0:
                    recs[n][h, 0, p - n * CAP] = out.astype(BF16)
                else:
                    send[h, g - 1, p] = out.astype(BF16)
        return 0

    n_cuts = len(cuts) - 1
    for k in range(n_cuts):
        lax.fori_loop(cuts[k], cuts[k + 1], functools.partial(place, cuts[k] // CAP), 0)
        for g in ORDER[:3]:
            for h in range(2):
                a_copy(h, g, k).start()

    for h in range(2):
        for d in range(1, SIDE):
            places_copy(h, d).wait()
    places_load = pltpu.make_async_copy(places, places_sm, sm_sem.at[1])
    places_load.start()
    places_load.wait()

    slot_cuts = (0, 5, 10, 15, SLOTS)
    n_slot_cuts = len(slot_cuts) - 1
    middle = 10

    def b_copy(h, off, q):
        cut = pl.ds(slot_cuts[q], slot_cuts[q + 1] - slot_cuts[q])
        k = off // 2
        return pltpu.make_async_remote_copy(
            part.at[h, off - 1, cut], got.at[h, 1 + k, cut], bsend.at[h, k, q], brecv.at[h, k, q],
            device_id=xy_peer(1 - h, off), device_id_type=MESH,
        )

    def via_copy(h, k):
        cut = pl.ds(middle * k, middle if k == 0 else SLOTS - middle)
        return pltpu.make_async_remote_copy(
            part.at[h, 1, cut], via.at[h, cut], vsend.at[h, k], vrecv.at[h, k],
            device_id=xy_peer(1 - h, 1 if k == 0 else SIDE - 1), device_id_type=MESH,
        )

    arrived = 0
    for n, off in enumerate(ORDER):
        needed = CAP * (n + 1)
        while cuts[arrived] < needed:
            for h in range(2):
                for g in range(1, SIDE):
                    a_copy(h, g, arrived).wait_recv()
            arrived += 1
        for h in range(2):
            ox = x if h == 0 else lax.rem(x + off, SIDE)
            oy = lax.rem(y + off, SIDE) if h == 0 else y

            def one(add, s, _, h=h, off=off, rec=recs[n], ox=ox, oy=oy):
                total = via[h, s].astype(F32) if add else jnp.zeros((TC, width), F32)
                for d in range(SIDE):
                    p = places_sm[h * SIDE + d, ox, 32 * oy + s]
                    there = jnp.where(p >= 0, F32(1.0), F32(0.0))
                    at = jnp.clip(p, 0, CAP - 1)
                    total = total + there * rec[h, d, at].astype(F32)
                if off == 0:
                    got[h, 0, s] = total.astype(BF16)
                else:
                    part[h, off - 1, s] = total.astype(BF16)
                return 0

            if off in (0, 2):
                lax.fori_loop(0, SLOTS, functools.partial(one, False), 0)
                if off:
                    via_copy(h, 0).start()
                    via_copy(h, 1).start()
            else:
                via_copy(h, off // 2).wait_recv()
                for q in range(n_slot_cuts):
                    add = (slot_cuts[q] < middle) == (off == 1)
                    lax.fori_loop(slot_cuts[q], slot_cuts[q + 1], functools.partial(one, add), 0)
                    b_copy(h, off, q).start()

    def z_copy(d, q):
        there = lax.rem(chan + d, n_chan)
        columns = pl.ds(pl.multiple_of(chan * 2 * width, 2 * width), 2 * width)
        cut = pl.ds(slot_cuts[q], slot_cuts[q + 1] - slot_cuts[q])
        if d == 0:
            return pltpu.make_async_copy(piece.at[there, cut], flat.at[cut, :, columns], zlocal.at[q])
        return pltpu.make_async_remote_copy(
            piece.at[there, cut], flat.at[cut, :, columns], zsend.at[d - 1, q], zrecv.at[d - 1, q],
            device_id=z_peer(d), device_id_type=MESH,
        )

    def one_slot(s, _):
        for h in range(2):
            total = got[h, 0, s].astype(F32) + got[h, 1, s].astype(F32) + got[h, 2, s].astype(F32)
            piece[:, s, :, h * width : (h + 1) * width] = total.astype(BF16).reshape(n_chan, rows, width)
        return 0

    for q in range(n_slot_cuts):
        for h in range(2):
            for off in (1, 3):
                b_copy(h, off, q).wait_recv()
        lax.fori_loop(slot_cuts[q], slot_cuts[q + 1], one_slot, 0)
        for d in (*range(1, n_chan), 0):
            z_copy(d, q).start()
    loads[0].wait()
    loads[1].wait()

    step = 256
    for lo_s, hi_s in ((0, middle), (middle, SLOTS)):
        for q in range(n_slot_cuts):
            if lo_s <= slot_cuts[q] < hi_s:
                z_copy(0, q).wait()
                for d in range(1, n_chan):
                    z_copy(d, q).wait_recv()
        v = flat[lo_s:hi_s].reshape((hi_s - lo_s) * rows, 2 * CH)
        for c in range(CH // step):
            lo = slice(c * step, (c + 1) * step)
            hi = slice(CH + c * step, CH + (c + 1) * step)
            re = jnp.dot(v, table[:, lo], preferred_element_type=F32).reshape(hi_s - lo_s, rows, step)
            im = jnp.dot(v, table[:, hi], preferred_element_type=F32).reshape(hi_s - lo_s, rows, step)
            cube[lo_s:hi_s, :, lo] = re.astype(BF16)
            cube[lo_s:hi_s, :, hi] = im.astype(BF16)
            product = re * galaxy[lo_s:hi_s, :, lo].astype(F32) + im * galaxy[lo_s:hi_s, :, hi].astype(F32)
            mine[lo_s:hi_s, lo] = jnp.sum(product, axis=1)

    share = CH // n_chan

    def share_columns(c):
        return pl.ds(pl.multiple_of(c * share, share), share)

    def p_copy(d):
        return pltpu.make_async_remote_copy(
            mine.at[:, share_columns(lax.rem(chan + d, n_chan))], shares.at[d - 1], psend.at[d - 1], precv.at[d - 1],
            device_id=z_peer(d), device_id_type=MESH,
        )

    def g_copy(d):
        own = total_power.at[:, share_columns(chan)]
        return pltpu.make_async_remote_copy(
            own, own, gsend.at[d - 1], grecv.at[d - 1], device_id=z_peer(d), device_id_type=MESH
        )

    for d in range(1, n_chan):
        p_copy(d).start()
    total = mine[:, share_columns(chan)]
    for d in range(1, n_chan):
        p_copy(d).wait_recv()
        total = total + shares[d - 1]
    total_power[:, share_columns(chan)] = total / F32(math.sqrt(TC))
    for d in range(1, n_chan):
        g_copy(d).start()
    for h in range(2):
        for g in range(1, SIDE):
            for k in range(n_cuts):
                a_copy(h, g, k).wait_send()
        for k in range(2):
            via_copy(h, k).wait_send()
            for q in range(n_slot_cuts):
                b_copy(h, 2 * k + 1, q).wait_send()
    for d in range(1, n_chan):
        for q in range(n_slot_cuts):
            z_copy(d, q).wait_send()
        p_copy(d).wait_send()
    for d in range(1, n_chan):
        g_copy(d).wait()
    power[...] = total_power[...]


def fused(n_chan, cuts, block_tile, tile_owner, tap_offset, cells, weight, vis, galaxy):
    nb, _, width = vis.shape
    n_cuts = len(cuts) - 1
    rows = TC // n_chan
    smem = pl.BlockSpec(memory_space=pltpu.SMEM)
    vmem = pl.BlockSpec(memory_space=pltpu.VMEM)
    hbm = pl.BlockSpec(memory_space=pl.ANY)
    dma = pltpu.SemaphoreType.DMA
    return pl.pallas_call(
        functools.partial(kernel, n_chan, cuts),
        out_shape=(
            jax.ShapeDtypeStruct((SLOTS, rows, 2 * CH), BF16),
            jax.ShapeDtypeStruct((SLOTS, CH), F32),
        ),
        in_specs=[vmem, vmem, smem, vmem, vmem, hbm, hbm, hbm],
        out_specs=(vmem, vmem),
        scratch_shapes=[
            pltpu.VMEM(vis.shape, BF16),
            pltpu.VMEM((4 * 2 * BR, width), F32),
            pltpu.VMEM((2 * CH, 2 * CH), BF16),
            pltpu.VMEM(galaxy.shape, BF16),
            pltpu.VMEM((8, 256), jnp.int32),
            pltpu.VMEM((8, 128), jnp.int32),
            pltpu.VMEM((2 * SIDE, 8, 128), jnp.int32),
            pltpu.SMEM((8, 128), jnp.int32),
            pltpu.SMEM((2 * SIDE, 8, 128), jnp.int32),
            pltpu.VMEM((2, SIDE, TC, width), F32),
            pltpu.VMEM((2, SIDE - 1, SIDE * CAP, TC, width), BF16),
            *[pltpu.VMEM((2, SIDE, CAP, TC, width), BF16) for _ in range(SIDE)],
            pltpu.VMEM((2, SIDE - 1, SLOTS, TC, width), BF16),
            pltpu.VMEM((2, SLOTS, TC, width), BF16),
            pltpu.VMEM((2, SIDE - 1, SLOTS, TC, width), BF16),
            pltpu.VMEM((n_chan, SLOTS, rows, 2 * width), BF16),
            pltpu.VMEM((SLOTS, rows, 2 * CH), BF16),
            pltpu.VMEM((SLOTS, CH), F32),
            pltpu.VMEM((n_chan - 1, SLOTS, CH // n_chan), F32),
            pltpu.VMEM((SLOTS, CH), F32),
            dma((6,)),
            dma((2 * SIDE,)),
            dma((2 * SIDE,)),
            dma((2,)),
            dma((2, SIDE - 1, n_cuts)),
            dma((2, SIDE - 1, n_cuts)),
            dma((2, 2, 4)),
            dma((2, 2, 4)),
            dma((2, 2)),
            dma((2, 2)),
            dma((n_chan - 1, 4)),
            dma((n_chan - 1, 4)),
            dma((4,)),
            dma((n_chan - 1,)),
            dma((n_chan - 1,)),
            dma((n_chan - 1,)),
            dma((n_chan - 1,)),
        ],
        compiler_params=pltpu.CompilerParams(collective_id=0, has_side_effects=True, vmem_limit_bytes=53 * MIB),
        name="grid_delay",
    )(
        block_tile.reshape(1, -1), tile_owner.reshape(1, -1), tap_offset, cells, weight,
        vis, jnp.asarray(table_constant(n_chan)), galaxy,
    )


def solution(mesh):
    n_chan = mesh.shape["chan"]

    def body(vis, row_cell, tap_weight, tap_offset, block_tile, tile_owner, galaxy):
        nb = block_tile.shape[0]
        blocks = vis.reshape(nb, 2 * BR, vis.shape[2])
        cells = row_cell.reshape(nb, 1, BR)
        weight = jnp.transpose(tap_weight.reshape(KT, nb, BR), (1, 0, 2)).astype(F32)
        return fused(
            n_chan, (0, 3, 11, 22, 33, 44), block_tile, tile_owner, tap_offset, cells, weight, blocks, galaxy
        )

    return jax.shard_map(
        body,
        mesh=mesh,
        in_specs=(
            P("uv", None, "chan"),
            P("uv"),
            P(None, "uv"),
            P(),
            P("uv"),
            P(),
            P("uv", "chan", None),
        ),
        out_specs=(P("uv", "chan", None), P("uv", None)),
        check_vma=False,
    )
```

```python
import functools
import math

import jax
import jax.numpy as jnp
import numpy as np
from jax import lax
from jax.experimental import pallas as pl
from jax.experimental.pallas import tpu as pltpu
from jax.sharding import PartitionSpec as P

MESH = pl.DeviceIdType.MESH
CH = 1024
BR = 128
TC = 128
KT = 8
N_OWN = 16
CAP = 11
SLOTS = 19
BLOCKS = 96
TILES = 160
SIDE = 4
ORDER = (2, 1, 3, 0)
F32 = jnp.float32
BF16 = jnp.bfloat16
MIB = 2**20


def table_constant(n_chan):
    freq = np.arange(CH, dtype=np.int64)
    phase = ((freq[:, None] * freq[None, :]) % CH).astype(np.float32) * np.float32(2.0 * math.pi / CH)
    cosine, sine = np.cos(phase), np.sin(phase)
    x = freq.astype(np.float32) * np.float32(2.0 * math.pi / CH)
    taper = (
        np.float32(0.35875)
        - np.float32(0.48829) * np.cos(x)
        + np.float32(0.14128) * np.cos(np.float32(2.0) * x)
        - np.float32(0.01168) * np.cos(np.float32(3.0) * x)
    )
    scale = (taper / np.float32(math.sqrt(CH)))[:, None]
    upper = np.concatenate([cosine * scale, -sine * scale], axis=1)
    lower = np.concatenate([sine * scale, cosine * scale], axis=1)
    table = np.stack([upper, lower]).reshape(2, n_chan, CH // n_chan, 2 * CH)
    return table.transpose(1, 0, 2, 3).reshape(2 * CH, 2 * CH).astype(jnp.bfloat16)


def peer(uv, chan, dx=0, dy=0):
    x = lax.rem(uv // SIDE + dx, SIDE)
    y = lax.rem(lax.rem(uv, SIDE) + dy, SIDE)
    return (x * SIDE + y, chan)


def column(row):
    return jnp.transpose(jnp.broadcast_to(row, (128, 128)))


def tall(row):
    return jnp.concatenate([column(row[:, :128]), column(row[:, 128:])], axis=0)


def position_in_order(d):
    return jnp.where(d == 2, 0, jnp.where(d == 1, 1, jnp.where(d == 3, 2, 3)))


def count(mask):
    return jnp.where(mask, 1, 0)


def make_tables(x, y, tb, lists, places):
    tile_r, own_r = tb[0:1, :128], tb[1:2, :]
    lane = lax.broadcasted_iota(jnp.int32, (128, 128), 1)
    sub = lax.broadcasted_iota(jnp.int32, (128, 128), 0)
    tile_c = column(tile_r)
    lane_t = lax.broadcasted_iota(jnp.int32, (256, 128), 1)
    t_c = lax.broadcasted_iota(jnp.int32, (256, 128), 0)
    own_c = tall(own_r)
    match = tile_r == t_c
    number_c = jnp.sum(count(match), axis=1, keepdims=True)
    number_r = [jnp.sum(count(tile_c == lane + 128 * i), axis=0, keepdims=True) for i in range(2)]
    same = [own_r[:, 128 * i : 128 * (i + 1)] == own_c for i in range(2)]
    rank_c = sum(jnp.sum(count(same[i] & (lane_t + 128 * i < t_c)), axis=1, keepdims=True) for i in range(2))
    earlier_r = jnp.sum(count((tile_c == tile_r) & (sub < lane)), axis=0, keepdims=True)
    repeat_c = count(column(earlier_r) > 0)
    dx_c, dy_c = ((own_c >> 2) - x) & 3, ((own_c & 3) - y) & 3
    slot_key = jnp.where(t_c < TILES, own_c * 32 + rank_c, -1)
    start_c = sum(
        jnp.sum(jnp.where(same[i] & (lane_t + 128 * i < t_c), number_r[i], 0), axis=1, keepdims=True) for i in range(2)
    )
    last_c = jnp.where(number_c > 0, start_c + number_c, 0)
    for i in range(4):
        hit = slot_key == lane_t + 128 * i
        places[i : i + 1, :] = jnp.sum(jnp.where(hit, last_c, 0), axis=0, keepdims=True) - 1
    for h in range(2):
        group_c, inner_c = (dx_c, dy_c) if h == 0 else (dy_c, dx_c)
        first_c = group_c * 64 + position_in_order(inner_c) * CAP + start_c
        key_r = jnp.sum(jnp.where(match, first_c, 0), axis=0, keepdims=True) + earlier_r
        key_c = column(jnp.where(lane[0:1] < BLOCKS, key_r, -1))
        for i in range(2):
            hit = key_c == lane + 128 * i
            row = 4 * h + i
            lists[row : row + 1, :] = jnp.sum(jnp.where(hit, sub, 0), axis=0, keepdims=True)
            lists[row + 2 : row + 3, :] = jnp.sum(jnp.where(hit, repeat_c, 0), axis=0, keepdims=True)


def kernel(
    n_chan, cuts,
    block_tile, tile_owner, tap_offset, cells, tap_weight, vis_hbm, table_hbm, galaxy_hbm,
    real, imag, power,
    vis, wide, weight, table, galaxy, tb, lists, places, lists_sm, places_sm, carry, send, rec0, rec1, rec2, rec3, part, via, got, piece, flat,
    mine, mine_sent, others,
    load_sem, msend, mrecv, sm_sem, asend, arecv, bsend, brecv, vsend, vrecv, zsend, zrecv, zlocal, psend, precv,
):
    uv, chan = lax.axis_index("uv"), lax.axis_index("chan")
    x, y = uv // SIDE, lax.rem(uv, SIDE)
    rows = TC // n_chan
    width = vis.shape[-1]
    recs = (rec0, rec1, rec2, rec3)

    def z_peer(d):
        return (uv, lax.rem(chan + d, n_chan))

    def xy_peer(h, d):
        return peer(uv, chan, dx=d) if h == 0 else peer(uv, chan, dy=d)

    loads = [
        pltpu.make_async_copy(table_hbm, table, load_sem.at[0]),
        pltpu.make_async_copy(galaxy_hbm, galaxy, load_sem.at[1]),
    ]
    quarter = BLOCKS // 4
    vis_loads = [
        pltpu.make_async_copy(
            vis_hbm.at[pl.ds(i * quarter, quarter)], vis.at[pl.ds(i * quarter, quarter)], load_sem.at[2 + i]
        )
        for i in range(4)
    ]
    for load in vis_loads:
        load.start()
    barrier = pltpu.get_barrier_semaphore()
    for h in range(2):
        for d in range(1, SIDE):
            pl.semaphore_signal(barrier, inc=1, device_id=xy_peer(h, d), device_id_type=MESH)
    for d in range(1, n_chan):
        pl.semaphore_signal(barrier, inc=1, device_id=z_peer(d), device_id_type=MESH)

    tb[...] = jnp.full(tb.shape, -1, jnp.int32)
    tb[0:1, 0 : block_tile.shape[1]] = block_tile[...]
    tb[1:2, 0 : tile_owner.shape[1]] = tile_owner[...]
    make_tables(x, y, tb, lists, places.at[0])
    places[SIDE] = places[0]
    to_scalars = pltpu.make_async_copy(lists, lists_sm, sm_sem.at[0])
    to_scalars.start()

    def split(i, _):
        for j in range(4):
            b = 4 * i + j
            weight[b] = tap_weight[:, pl.ds(pl.multiple_of(b * BR, BR), BR)].astype(F32)
            wide[2 * BR * j : 2 * BR * (j + 1), :] = vis[b].astype(F32)
            for part_of in range(2):
                rows_of = wide[pl.ds(2 * BR * j + part_of, BR, stride=2), :]
                vis[b, BR * part_of : BR * (part_of + 1), :] = rows_of.astype(BF16)
        return 0

    for i, load in enumerate(vis_loads):
        load.wait()
        lax.fori_loop(i * quarter // 4, (i + 1) * quarter // 4, split, 0)
    pl.semaphore_wait(barrier, 2 * (SIDE - 1) + n_chan - 1)

    def places_copy(h, d):
        k = h * SIDE + d
        return pltpu.make_async_remote_copy(
            places.at[0], places.at[k], msend.at[k], mrecv.at[k], device_id=xy_peer(h, d), device_id_type=MESH
        )

    for h in range(2):
        for d in range(1, SIDE):
            if h == 0:
                places_copy(h, d).start()
    for d in range(1, SIDE):
        places_copy(1, d).start()
    carry[...] = jnp.zeros_like(carry)
    mine_sent[...] = jnp.zeros_like(mine_sent)
    to_scalars.wait()
    loads[0].start()
    loads[1].start()

    def a_copy(h, g, k):
        n, size = cuts[k] // CAP, cuts[k + 1] - cuts[k]
        return pltpu.make_async_remote_copy(
            send.at[h, g - 1, pl.ds(cuts[k], size)], recs[n].at[h, g, pl.ds(cuts[k] - n * CAP, size)], asend.at[h, g - 1, k], arecv.at[h, g - 1, k],
            device_id=xy_peer(h, g), device_id_type=MESH,
        )

    cell_rows = lax.broadcasted_iota(jnp.int32, (TC, BR), 0)

    def place(n, p, _):
        for g in ORDER:
            for h in range(2):
                row, at = 4 * h + g // 2, 64 * (g % 2) + p
                b = jnp.minimum(lists_sm[row, at], BLOCKS - 1)
                keep = lists_sm[row + 2, at].astype(F32)
                away = cell_rows - cells[b]
                w = weight[b]
                matrix = jnp.zeros((TC, BR), F32)
                for k in range(KT):
                    matrix = matrix + jnp.where(away == tap_offset[k], w[k : k + 1, :], 0.0)
                half = vis[b, BR * h : BR * (h + 1), :]
                out = jnp.dot(matrix.astype(BF16), half, preferred_element_type=F32)
                out = out + keep * carry[h, g]
                carry[h, g] = out
                if g == 0:
                    recs[n][h, 0, p - n * CAP] = out.astype(BF16)
                else:
                    send[h, g - 1, p] = out.astype(BF16)
        return 0

    n_cuts = len(cuts) - 1
    for k in range(n_cuts):
        lax.fori_loop(cuts[k], cuts[k + 1], functools.partial(place, cuts[k] // CAP), 0)
        for g in ORDER[:3]:
            for h in range(2):
                a_copy(h, g, k).start()

    for h in range(2):
        for d in range(1, SIDE):
            places_copy(h, d).wait()
    places_load = pltpu.make_async_copy(places, places_sm, sm_sem.at[1])
    places_load.start()
    places_load.wait()

    slot_cuts = (0, 5, 10, 15, SLOTS)
    n_slot_cuts = len(slot_cuts) - 1
    middle = 10

    def b_copy(h, off, q):
        cut = pl.ds(slot_cuts[q], slot_cuts[q + 1] - slot_cuts[q])
        k = off // 2
        return pltpu.make_async_remote_copy(
            part.at[h, off - 1, cut], got.at[h, 1 + k, cut], bsend.at[h, k, q], brecv.at[h, k, q],
            device_id=xy_peer(1 - h, off), device_id_type=MESH,
        )

    def via_copy(h, k):
        cut = pl.ds(middle * k, middle if k == 0 else SLOTS - middle)
        return pltpu.make_async_remote_copy(
            part.at[h, 1, cut], via.at[h, cut], vsend.at[h, k], vrecv.at[h, k],
            device_id=xy_peer(1 - h, 1 if k == 0 else SIDE - 1), device_id_type=MESH,
        )

    arrived = 0
    for n, off in enumerate(ORDER):
        needed = CAP * (n + 1)
        while cuts[arrived] < needed:
            for h in range(2):
                for g in range(1, SIDE):
                    a_copy(h, g, arrived).wait_recv()
            arrived += 1
        for h in range(2):
            ox = x if h == 0 else lax.rem(x + off, SIDE)
            oy = lax.rem(y + off, SIDE) if h == 0 else y

            def one(add, s, _, h=h, off=off, rec=recs[n], ox=ox, oy=oy):
                total = via[h, s].astype(F32) if add else jnp.zeros((TC, width), F32)
                for d in range(SIDE):
                    p = places_sm[h * SIDE + d, ox, 32 * oy + s]
                    there = jnp.where(p >= 0, F32(1.0), F32(0.0))
                    at = jnp.clip(p, 0, CAP - 1)
                    total = total + there * rec[h, d, at].astype(F32)
                if off == 0:
                    got[h, 0, s] = total.astype(BF16)
                else:
                    part[h, off - 1, s] = total.astype(BF16)
                return 0

            if off in (0, 2):
                lax.fori_loop(0, SLOTS, functools.partial(one, False), 0)
                if off:
                    via_copy(h, 0).start()
                    via_copy(h, 1).start()
            else:
                via_copy(h, off // 2).wait_recv()
                for q in range(n_slot_cuts):
                    add = (slot_cuts[q] < middle) == (off == 1)
                    lax.fori_loop(slot_cuts[q], slot_cuts[q + 1], functools.partial(one, add), 0)
                    b_copy(h, off, q).start()

    def z_copy(d, q):
        there = lax.rem(chan + d, n_chan)
        columns = pl.ds(pl.multiple_of(chan * 2 * width, 2 * width), 2 * width)
        cut = pl.ds(slot_cuts[q], slot_cuts[q + 1] - slot_cuts[q])
        if d == 0:
            return pltpu.make_async_copy(piece.at[there, cut], flat.at[cut, :, columns], zlocal.at[q])
        return pltpu.make_async_remote_copy(
            piece.at[there, cut], flat.at[cut, :, columns], zsend.at[d - 1, q], zrecv.at[d - 1, q],
            device_id=z_peer(d), device_id_type=MESH,
        )

    def one_slot(s, _):
        for h in range(2):
            total = got[h, 0, s].astype(F32) + got[h, 1, s].astype(F32) + got[h, 2, s].astype(F32)
            piece[:, s, :, h * width : (h + 1) * width] = total.astype(BF16).reshape(n_chan, rows, width)
        return 0

    for q in range(n_slot_cuts):
        for h in range(2):
            for off in (1, 3):
                b_copy(h, off, q).wait_recv()
        lax.fori_loop(slot_cuts[q], slot_cuts[q + 1], one_slot, 0)
        for d in (*range(1, n_chan), 0):
            z_copy(d, q).start()
    loads[0].wait()
    loads[1].wait()

    step = 256
    def p_copy(d, i):
        return pltpu.make_async_remote_copy(
            mine_sent.at[i], others.at[d - 1, i], psend.at[d - 1, i], precv.at[d - 1, i],
            device_id=z_peer(d), device_id_type=MESH,
        )

    parts = ((0, middle), (middle, SLOTS))
    for i, (lo_s, hi_s) in enumerate(parts):
        for q in range(n_slot_cuts):
            if lo_s <= slot_cuts[q] < hi_s:
                z_copy(0, q).wait()
                for d in range(1, n_chan):
                    z_copy(d, q).wait_recv()
        v = flat[lo_s:hi_s].reshape((hi_s - lo_s) * rows, 2 * CH)
        for c in range(CH // step):
            lo = slice(c * step, (c + 1) * step)
            hi = slice(CH + c * step, CH + (c + 1) * step)
            re = jnp.dot(v, table[:, lo], preferred_element_type=F32).reshape(hi_s - lo_s, rows, step)
            im = jnp.dot(v, table[:, hi], preferred_element_type=F32).reshape(hi_s - lo_s, rows, step)
            real[lo_s:hi_s, :, lo] = re.astype(BF16)
            imag[lo_s:hi_s, :, lo] = im.astype(BF16)
            product = re * galaxy[lo_s:hi_s, :, lo].astype(F32) + im * galaxy[lo_s:hi_s, :, hi].astype(F32)
            sums = jnp.sum(product, axis=1)
            mine[lo_s:hi_s, lo] = sums
            mine_sent[i, 0 : hi_s - lo_s, lo] = sums.astype(BF16)
        for d in range(1, n_chan):
            p_copy(d, i).start()

    for h in range(2):
        for g in range(1, SIDE):
            for k in range(n_cuts):
                a_copy(h, g, k).wait_send()
        for k in range(2):
            via_copy(h, k).wait_send()
            for q in range(n_slot_cuts):
                b_copy(h, 2 * k + 1, q).wait_send()
    for d in range(1, n_chan):
        for q in range(n_slot_cuts):
            z_copy(d, q).wait_send()
        for i in range(2):
            p_copy(d, i).wait_send()
    for i, (lo_s, hi_s) in enumerate(parts):
        total = mine[lo_s:hi_s, :]
        for d in range(1, n_chan):
            p_copy(d, i).wait_recv()
            total = total + others[d - 1, i, 0 : hi_s - lo_s, :].astype(F32)
        power[lo_s:hi_s, :] = total


def fused(n_chan, cuts, block_tile, tile_owner, tap_offset, cells, weight, vis, galaxy):
    nb, _, width = vis.shape
    n_cuts = len(cuts) - 1
    rows = TC // n_chan
    smem = pl.BlockSpec(memory_space=pltpu.SMEM)
    vmem = pl.BlockSpec(memory_space=pltpu.VMEM)
    hbm = pl.BlockSpec(memory_space=pl.ANY)
    dma = pltpu.SemaphoreType.DMA
    return pl.pallas_call(
        functools.partial(kernel, n_chan, cuts),
        out_shape=(
            jax.ShapeDtypeStruct((SLOTS, rows, CH), BF16),
            jax.ShapeDtypeStruct((SLOTS, rows, CH), BF16),
            jax.ShapeDtypeStruct((SLOTS, CH), F32),
        ),
        in_specs=[vmem, vmem, smem, vmem, vmem, hbm, hbm, hbm],
        out_specs=(vmem, vmem, vmem),
        scratch_shapes=[
            pltpu.VMEM(vis.shape, BF16),
            pltpu.VMEM((4 * 2 * BR, width), F32),
            pltpu.VMEM((nb, KT, BR), F32),
            pltpu.VMEM((2 * CH, 2 * CH), BF16),
            pltpu.VMEM(galaxy.shape, BF16),
            pltpu.VMEM((8, 256), jnp.int32),
            pltpu.VMEM((8, 128), jnp.int32),
            pltpu.VMEM((2 * SIDE, 8, 128), jnp.int32),
            pltpu.SMEM((8, 128), jnp.int32),
            pltpu.SMEM((2 * SIDE, 8, 128), jnp.int32),
            pltpu.VMEM((2, SIDE, TC, width), F32),
            pltpu.VMEM((2, SIDE - 1, SIDE * CAP, TC, width), BF16),
            *[pltpu.VMEM((2, SIDE, CAP, TC, width), BF16) for _ in range(SIDE)],
            pltpu.VMEM((2, SIDE - 1, SLOTS, TC, width), BF16),
            pltpu.VMEM((2, SLOTS, TC, width), BF16),
            pltpu.VMEM((2, SIDE - 1, SLOTS, TC, width), BF16),
            pltpu.VMEM((n_chan, SLOTS, rows, 2 * width), BF16),
            pltpu.VMEM((SLOTS, rows, 2 * CH), BF16),
            pltpu.VMEM((SLOTS, CH), F32),
            pltpu.VMEM((2, 16, CH), BF16),
            pltpu.VMEM((n_chan - 1, 2, 16, CH), BF16),
            dma((6,)),
            dma((2 * SIDE,)),
            dma((2 * SIDE,)),
            dma((2,)),
            dma((2, SIDE - 1, n_cuts)),
            dma((2, SIDE - 1, n_cuts)),
            dma((2, 2, 4)),
            dma((2, 2, 4)),
            dma((2, 2)),
            dma((2, 2)),
            dma((n_chan - 1, 4)),
            dma((n_chan - 1, 4)),
            dma((4,)),
            dma((n_chan - 1, 2)),
            dma((n_chan - 1, 2)),
        ],
        compiler_params=pltpu.CompilerParams(collective_id=0, has_side_effects=True, vmem_limit_bytes=60 * MIB),
        name="grid_delay",
    )(
        block_tile.reshape(1, -1), tile_owner.reshape(1, -1), tap_offset, cells, weight,
        vis, jnp.asarray(table_constant(n_chan)), galaxy,
    )


def solution(mesh):
    n_chan = mesh.shape["chan"]

    def body(vis, row_cell, tap_weight, tap_offset, block_tile, tile_owner, galaxy):
        nb = block_tile.shape[0]
        blocks = vis.reshape(nb, 2 * BR, vis.shape[2])
        cells = row_cell.reshape(nb, 1, BR)
        real, imag, power = fused(
            n_chan, (0, 1, 4, 11, 22, 33, 44), block_tile, tile_owner, tap_offset, cells, tap_weight, blocks, galaxy
        )
        return jnp.concatenate([real, imag], axis=-1), power / F32(math.sqrt(TC))

    return jax.shard_map(
        body,
        mesh=mesh,
        in_specs=(
            P("uv", None, "chan"),
            P("uv"),
            P(None, "uv"),
            P(),
            P("uv"),
            P(),
            P("uv", "chan", None),
        ),
        out_specs=(P("uv", "chan", None), P("uv", None)),
        check_vma=False,
    )
```

```python
import functools
import math

import jax
import jax.numpy as jnp
import numpy as np
from jax import lax
from jax.experimental import pallas as pl
from jax.experimental.pallas import tpu as pltpu
from jax.sharding import PartitionSpec as P

MESH = pl.DeviceIdType.MESH
CH = 1024
BR = 128
TC = 128
KT = 8
N_OWN = 16
CAP = 11
SLOTS = 19
BLOCKS = 96
TILES = 160
SIDE = 4
ORDER = (2, 1, 3, 0)
F32 = jnp.float32
BF16 = jnp.bfloat16
MIB = 2**20


def table_constant(n_chan):
    freq = np.arange(CH, dtype=np.int64)
    phase = ((freq[:, None] * freq[None, :]) % CH).astype(np.float32) * np.float32(2.0 * math.pi / CH)
    cosine, sine = np.cos(phase), np.sin(phase)
    x = freq.astype(np.float32) * np.float32(2.0 * math.pi / CH)
    taper = (
        np.float32(0.35875)
        - np.float32(0.48829) * np.cos(x)
        + np.float32(0.14128) * np.cos(np.float32(2.0) * x)
        - np.float32(0.01168) * np.cos(np.float32(3.0) * x)
    )
    scale = (taper / np.float32(math.sqrt(CH)))[:, None]
    upper = np.concatenate([cosine * scale, -sine * scale], axis=1)
    lower = np.concatenate([sine * scale, cosine * scale], axis=1)
    table = np.stack([upper, lower]).reshape(2, n_chan, CH // n_chan, 2 * CH)
    return table.transpose(1, 0, 2, 3).reshape(2 * CH, 2 * CH).astype(jnp.bfloat16)


def peer(uv, chan, dx=0, dy=0):
    x = lax.rem(uv // SIDE + dx, SIDE)
    y = lax.rem(lax.rem(uv, SIDE) + dy, SIDE)
    return (x * SIDE + y, chan)


def column(row):
    return jnp.transpose(jnp.broadcast_to(row, (128, 128)))


def tall(row):
    return jnp.concatenate([column(row[:, :128]), column(row[:, 128:])], axis=0)


def position_in_order(d):
    return jnp.where(d == 2, 0, jnp.where(d == 1, 1, jnp.where(d == 3, 2, 3)))


def count(mask):
    return jnp.where(mask, 1, 0)


def make_tables(x, y, tb, lists, places):
    tile_r, own_r = tb[0:1, :128], tb[1:2, :]
    lane = lax.broadcasted_iota(jnp.int32, (128, 128), 1)
    sub = lax.broadcasted_iota(jnp.int32, (128, 128), 0)
    tile_c = column(tile_r)
    lane_t = lax.broadcasted_iota(jnp.int32, (256, 128), 1)
    t_c = lax.broadcasted_iota(jnp.int32, (256, 128), 0)
    own_c = tall(own_r)
    match = tile_r == t_c
    number_c = jnp.sum(count(match), axis=1, keepdims=True)
    number_r = [jnp.sum(count(tile_c == lane + 128 * i), axis=0, keepdims=True) for i in range(2)]
    same = [own_r[:, 128 * i : 128 * (i + 1)] == own_c for i in range(2)]
    rank_c = sum(jnp.sum(count(same[i] & (lane_t + 128 * i < t_c)), axis=1, keepdims=True) for i in range(2))
    earlier_r = jnp.sum(count((tile_c == tile_r) & (sub < lane)), axis=0, keepdims=True)
    repeat_c = count(column(earlier_r) > 0)
    dx_c, dy_c = ((own_c >> 2) - x) & 3, ((own_c & 3) - y) & 3
    slot_key = jnp.where(t_c < TILES, own_c * 32 + rank_c, -1)
    start_c = sum(
        jnp.sum(jnp.where(same[i] & (lane_t + 128 * i < t_c), number_r[i], 0), axis=1, keepdims=True) for i in range(2)
    )
    last_c = jnp.where(number_c > 0, start_c + number_c, 0)
    for i in range(4):
        hit = slot_key == lane_t + 128 * i
        places[i : i + 1, :] = jnp.sum(jnp.where(hit, last_c, 0), axis=0, keepdims=True) - 1
    for h in range(2):
        group_c, inner_c = (dx_c, dy_c) if h == 0 else (dy_c, dx_c)
        first_c = group_c * 64 + position_in_order(inner_c) * CAP + start_c
        key_r = jnp.sum(jnp.where(match, first_c, 0), axis=0, keepdims=True) + earlier_r
        key_c = column(jnp.where(lane[0:1] < BLOCKS, key_r, -1))
        for i in range(2):
            hit = key_c == lane + 128 * i
            row = 4 * h + i
            lists[row : row + 1, :] = jnp.sum(jnp.where(hit, sub, 0), axis=0, keepdims=True)
            lists[row + 2 : row + 3, :] = jnp.sum(jnp.where(hit, repeat_c, 0), axis=0, keepdims=True)


def kernel(
    n_chan, cuts,
    block_tile, tile_owner, tap_offset, cells, tap_weight, vis_hbm, table_hbm, galaxy_hbm,
    real, imag, power,
    vis, wide, weight, table, galaxy, tb, lists, places, lists_sm, places_sm, carry, send, rec0, rec1, rec2, rec3, part, via, got, piece, flat,
    mine, mine_sent, others, last_sent, last_others,
    load_sem, msend, mrecv, sm_sem, asend, arecv, bsend, brecv, vsend, vrecv, zsend, zrecv, zlocal, psend, precv,
):
    uv, chan = lax.axis_index("uv"), lax.axis_index("chan")
    x, y = uv // SIDE, lax.rem(uv, SIDE)
    rows = TC // n_chan
    width = vis.shape[-1]
    recs = (rec0, rec1, rec2, rec3)

    def z_peer(d):
        return (uv, lax.rem(chan + d, n_chan))

    def xy_peer(h, d):
        return peer(uv, chan, dx=d) if h == 0 else peer(uv, chan, dy=d)

    loads = [
        pltpu.make_async_copy(table_hbm, table, load_sem.at[0]),
        pltpu.make_async_copy(galaxy_hbm, galaxy, load_sem.at[1]),
    ]
    quarter = BLOCKS // 4
    vis_loads = [
        pltpu.make_async_copy(
            vis_hbm.at[pl.ds(i * quarter, quarter)], vis.at[pl.ds(i * quarter, quarter)], load_sem.at[2 + i]
        )
        for i in range(4)
    ]
    for load in vis_loads:
        load.start()
    barrier = pltpu.get_barrier_semaphore()
    for h in range(2):
        for d in range(1, SIDE):
            pl.semaphore_signal(barrier, inc=1, device_id=xy_peer(h, d), device_id_type=MESH)
    for d in range(1, n_chan):
        pl.semaphore_signal(barrier, inc=1, device_id=z_peer(d), device_id_type=MESH)

    tb[...] = jnp.full(tb.shape, -1, jnp.int32)
    tb[0:1, 0 : block_tile.shape[1]] = block_tile[...]
    tb[1:2, 0 : tile_owner.shape[1]] = tile_owner[...]
    make_tables(x, y, tb, lists, places.at[0])
    places[SIDE] = places[0]
    to_scalars = pltpu.make_async_copy(lists, lists_sm, sm_sem.at[0])
    to_scalars.start()

    def split(i, _):
        for j in range(4):
            b = 4 * i + j
            weight[b] = tap_weight[:, pl.ds(pl.multiple_of(b * BR, BR), BR)].astype(F32)
            wide[2 * BR * j : 2 * BR * (j + 1), :] = vis[b].astype(F32)
            for part_of in range(2):
                rows_of = wide[pl.ds(2 * BR * j + part_of, BR, stride=2), :]
                vis[b, BR * part_of : BR * (part_of + 1), :] = rows_of.astype(BF16)
        return 0

    for i, load in enumerate(vis_loads):
        load.wait()
        lax.fori_loop(i * quarter // 4, (i + 1) * quarter // 4, split, 0)
    pl.semaphore_wait(barrier, 2 * (SIDE - 1) + n_chan - 1)

    def places_copy(h, d):
        k = h * SIDE + d
        return pltpu.make_async_remote_copy(
            places.at[0], places.at[k], msend.at[k], mrecv.at[k], device_id=xy_peer(h, d), device_id_type=MESH
        )

    for h in range(2):
        for d in range(1, SIDE):
            if h == 0:
                places_copy(h, d).start()
    for d in range(1, SIDE):
        places_copy(1, d).start()
    carry[...] = jnp.zeros_like(carry)
    mine_sent[...] = jnp.zeros_like(mine_sent)
    to_scalars.wait()
    loads[0].start()
    loads[1].start()

    def a_copy(h, g, k):
        n, size = cuts[k] // CAP, cuts[k + 1] - cuts[k]
        return pltpu.make_async_remote_copy(
            send.at[h, g - 1, pl.ds(cuts[k], size)], recs[n].at[h, g, pl.ds(cuts[k] - n * CAP, size)], asend.at[h, g - 1, k], arecv.at[h, g - 1, k],
            device_id=xy_peer(h, g), device_id_type=MESH,
        )

    cell_rows = lax.broadcasted_iota(jnp.int32, (TC, BR), 0)

    def place(n, p, _):
        for g in ORDER:
            for h in range(2):
                row, at = 4 * h + g // 2, 64 * (g % 2) + p
                b = jnp.minimum(lists_sm[row, at], BLOCKS - 1)
                keep = lists_sm[row + 2, at].astype(F32)
                away = cell_rows - cells[b]
                w = weight[b]
                matrix = jnp.zeros((TC, BR), F32)
                for k in range(KT):
                    matrix = matrix + jnp.where(away == tap_offset[k], w[k : k + 1, :], 0.0)
                half = vis[b, BR * h : BR * (h + 1), :]
                out = jnp.dot(matrix.astype(BF16), half, preferred_element_type=F32)
                out = out + keep * carry[h, g]
                carry[h, g] = out
                if g == 0:
                    recs[n][h, 0, p - n * CAP] = out.astype(BF16)
                else:
                    send[h, g - 1, p] = out.astype(BF16)
        return 0

    n_cuts = len(cuts) - 1
    for k in range(n_cuts):
        lax.fori_loop(cuts[k], cuts[k + 1], functools.partial(place, cuts[k] // CAP), 0)
        for g in ORDER[:3]:
            for h in range(2):
                a_copy(h, g, k).start()

    for h in range(2):
        for d in range(1, SIDE):
            places_copy(h, d).wait()
    places_load = pltpu.make_async_copy(places, places_sm, sm_sem.at[1])
    places_load.start()
    places_load.wait()

    slot_cuts = (0, 5, 10, 15, SLOTS)
    n_slot_cuts = len(slot_cuts) - 1
    middle = 10

    def b_copy(h, off, q):
        cut = pl.ds(slot_cuts[q], slot_cuts[q + 1] - slot_cuts[q])
        k = off // 2
        return pltpu.make_async_remote_copy(
            part.at[h, off - 1, cut], got.at[h, 1 + k, cut], bsend.at[h, k, q], brecv.at[h, k, q],
            device_id=xy_peer(1 - h, off), device_id_type=MESH,
        )

    def via_copy(h, k):
        cut = pl.ds(middle * k, middle if k == 0 else SLOTS - middle)
        return pltpu.make_async_remote_copy(
            part.at[h, 1, cut], via.at[h, cut], vsend.at[h, k], vrecv.at[h, k],
            device_id=xy_peer(1 - h, 1 if k == 0 else SIDE - 1), device_id_type=MESH,
        )

    arrived = 0
    for n, off in enumerate(ORDER):
        needed = CAP * (n + 1)
        while cuts[arrived] < needed:
            for h in range(2):
                for g in range(1, SIDE):
                    a_copy(h, g, arrived).wait_recv()
            arrived += 1
        for h in range(2):
            ox = x if h == 0 else lax.rem(x + off, SIDE)
            oy = lax.rem(y + off, SIDE) if h == 0 else y

            def one(add, s, _, h=h, off=off, rec=recs[n], ox=ox, oy=oy):
                total = via[h, s].astype(F32) if add else jnp.zeros((TC, width), F32)
                for d in range(SIDE):
                    p = places_sm[h * SIDE + d, ox, 32 * oy + s]
                    there = jnp.where(p >= 0, F32(1.0), F32(0.0))
                    at = jnp.clip(p, 0, CAP - 1)
                    total = total + there * rec[h, d, at].astype(F32)
                if off == 0:
                    got[h, 0, s] = total.astype(BF16)
                else:
                    part[h, off - 1, s] = total.astype(BF16)
                return 0

            if off in (0, 2):
                lax.fori_loop(0, SLOTS, functools.partial(one, False), 0)
                if off:
                    via_copy(h, 0).start()
                    via_copy(h, 1).start()
            else:
                via_copy(h, off // 2).wait_recv()
                for q in range(n_slot_cuts):
                    add = (slot_cuts[q] < middle) == (off == 1)
                    lax.fori_loop(slot_cuts[q], slot_cuts[q + 1], functools.partial(one, add), 0)
                    b_copy(h, off, q).start()

    def z_copy(d, q):
        there = lax.rem(chan + d, n_chan)
        columns = pl.ds(pl.multiple_of(chan * 2 * width, 2 * width), 2 * width)
        cut = pl.ds(slot_cuts[q], slot_cuts[q + 1] - slot_cuts[q])
        if d == 0:
            return pltpu.make_async_copy(piece.at[there, cut], flat.at[cut, :, columns], zlocal.at[q])
        return pltpu.make_async_remote_copy(
            piece.at[there, cut], flat.at[cut, :, columns], zsend.at[d - 1, q], zrecv.at[d - 1, q],
            device_id=z_peer(d), device_id_type=MESH,
        )

    def one_slot(s, _):
        for h in range(2):
            total = got[h, 0, s].astype(F32) + got[h, 1, s].astype(F32) + got[h, 2, s].astype(F32)
            piece[:, s, :, h * width : (h + 1) * width] = total.astype(BF16).reshape(n_chan, rows, width)
        return 0

    for q in range(n_slot_cuts):
        for h in range(2):
            for off in (1, 3):
                b_copy(h, off, q).wait_recv()
        lax.fori_loop(slot_cuts[q], slot_cuts[q + 1], one_slot, 0)
        for d in (*range(1, n_chan), 0):
            z_copy(d, q).start()
    loads[0].wait()
    loads[1].wait()

    step = 256
    def p_copy(d, i):
        return pltpu.make_async_remote_copy(
            (mine_sent, last_sent)[i], (others, last_others)[i].at[d - 1], psend.at[d - 1, i], precv.at[d - 1, i],
            device_id=z_peer(d), device_id_type=MESH,
        )

    parts = ((0, slot_cuts[-2]), (slot_cuts[-2], SLOTS))
    for i, (lo_s, hi_s) in enumerate(parts):
        for q in range(n_slot_cuts):
            if lo_s <= slot_cuts[q] < hi_s:
                z_copy(0, q).wait()
                for d in range(1, n_chan):
                    z_copy(d, q).wait_recv()
        v = flat[lo_s:hi_s].reshape((hi_s - lo_s) * rows, 2 * CH)
        for c in range(CH // step):
            lo = slice(c * step, (c + 1) * step)
            hi = slice(CH + c * step, CH + (c + 1) * step)
            re = jnp.dot(v, table[:, lo], preferred_element_type=F32).reshape(hi_s - lo_s, rows, step)
            im = jnp.dot(v, table[:, hi], preferred_element_type=F32).reshape(hi_s - lo_s, rows, step)
            real[lo_s:hi_s, :, lo] = re.astype(BF16)
            imag[lo_s:hi_s, :, lo] = im.astype(BF16)
            product = re * galaxy[lo_s:hi_s, :, lo].astype(F32) + im * galaxy[lo_s:hi_s, :, hi].astype(F32)
            sums = jnp.sum(product, axis=1)
            mine[lo_s:hi_s, lo] = sums
            if i == 0:
                mine_sent[0 : hi_s - lo_s, lo] = sums.astype(BF16)
            else:
                last_sent[4 * c : 4 * c + 4, :] = sums.astype(BF16)
        for d in range(1, n_chan):
            p_copy(d, i).start()

    for h in range(2):
        for g in range(1, SIDE):
            for k in range(n_cuts):
                a_copy(h, g, k).wait_send()
        for k in range(2):
            via_copy(h, k).wait_send()
            for q in range(n_slot_cuts):
                b_copy(h, 2 * k + 1, q).wait_send()
    for d in range(1, n_chan):
        for q in range(n_slot_cuts):
            z_copy(d, q).wait_send()
        for i in range(2):
            p_copy(d, i).wait_send()
    first = slot_cuts[-2]
    total = mine[:first, :]
    for d in range(1, n_chan):
        p_copy(d, 0).wait_recv()
        total = total + others[d - 1, :first, :].astype(F32)
    power[:first, :] = total / F32(math.sqrt(TC))
    for d in range(1, n_chan):
        p_copy(d, 1).wait_recv()
    for c in range(CH // step):
        columns = slice(c * step, (c + 1) * step)
        total = mine[first:, columns]
        for d in range(1, n_chan):
            total = total + last_others[d - 1, 4 * c : 4 * c + 4, :].astype(F32)
        power[first:, columns] = total / F32(math.sqrt(TC))


def fused(n_chan, cuts, block_tile, tile_owner, tap_offset, cells, weight, vis, galaxy):
    nb, _, width = vis.shape
    n_cuts = len(cuts) - 1
    rows = TC // n_chan
    smem = pl.BlockSpec(memory_space=pltpu.SMEM)
    vmem = pl.BlockSpec(memory_space=pltpu.VMEM)
    hbm = pl.BlockSpec(memory_space=pl.ANY)
    dma = pltpu.SemaphoreType.DMA
    return pl.pallas_call(
        functools.partial(kernel, n_chan, cuts),
        out_shape=(
            jax.ShapeDtypeStruct((SLOTS, rows, CH), BF16),
            jax.ShapeDtypeStruct((SLOTS, rows, CH), BF16),
            jax.ShapeDtypeStruct((SLOTS, CH), F32),
        ),
        in_specs=[vmem, vmem, smem, vmem, vmem, hbm, hbm, hbm],
        out_specs=(vmem, vmem, vmem),
        scratch_shapes=[
            pltpu.VMEM(vis.shape, BF16),
            pltpu.VMEM((4 * 2 * BR, width), F32),
            pltpu.VMEM((nb, KT, BR), F32),
            pltpu.VMEM((2 * CH, 2 * CH), BF16),
            pltpu.VMEM(galaxy.shape, BF16),
            pltpu.VMEM((8, 256), jnp.int32),
            pltpu.VMEM((8, 128), jnp.int32),
            pltpu.VMEM((2 * SIDE, 8, 128), jnp.int32),
            pltpu.SMEM((8, 128), jnp.int32),
            pltpu.SMEM((2 * SIDE, 8, 128), jnp.int32),
            pltpu.VMEM((2, SIDE, TC, width), F32),
            pltpu.VMEM((2, SIDE - 1, SIDE * CAP, TC, width), BF16),
            *[pltpu.VMEM((2, SIDE, CAP, TC, width), BF16) for _ in range(SIDE)],
            pltpu.VMEM((2, SIDE - 1, SLOTS, TC, width), BF16),
            pltpu.VMEM((2, SLOTS, TC, width), BF16),
            pltpu.VMEM((2, SIDE - 1, SLOTS, TC, width), BF16),
            pltpu.VMEM((n_chan, SLOTS, rows, 2 * width), BF16),
            pltpu.VMEM((SLOTS, rows, 2 * CH), BF16),
            pltpu.VMEM((SLOTS, CH), F32),
            pltpu.VMEM((16, CH), BF16),
            pltpu.VMEM((n_chan - 1, 16, CH), BF16),
            pltpu.VMEM((16, CH // 4), BF16),
            pltpu.VMEM((n_chan - 1, 16, CH // 4), BF16),
            dma((6,)),
            dma((2 * SIDE,)),
            dma((2 * SIDE,)),
            dma((2,)),
            dma((2, SIDE - 1, n_cuts)),
            dma((2, SIDE - 1, n_cuts)),
            dma((2, 2, 4)),
            dma((2, 2, 4)),
            dma((2, 2)),
            dma((2, 2)),
            dma((n_chan - 1, 4)),
            dma((n_chan - 1, 4)),
            dma((4,)),
            dma((n_chan - 1, 2)),
            dma((n_chan - 1, 2)),
        ],
        compiler_params=pltpu.CompilerParams(collective_id=0, has_side_effects=True, vmem_limit_bytes=60 * MIB),
        name="grid_delay",
    )(
        block_tile.reshape(1, -1), tile_owner.reshape(1, -1), tap_offset, cells, weight,
        vis, jnp.asarray(table_constant(n_chan)), galaxy,
    )


def outputs_kernel(real, imag, power, cube, power_out, sem):
    copies = [
        pltpu.make_async_copy(real, cube.at[:, :, pl.ds(0, CH)], sem.at[0]),
        pltpu.make_async_copy(imag, cube.at[:, :, pl.ds(CH, CH)], sem.at[1]),
        pltpu.make_async_copy(power, power_out, sem.at[2]),
    ]
    for copy in copies:
        copy.start()
    for copy in copies:
        copy.wait()


def outputs(real, imag, power):
    hbm = pl.BlockSpec(memory_space=pl.ANY)
    return pl.pallas_call(
        outputs_kernel,
        out_shape=(
            jax.ShapeDtypeStruct((*real.shape[:2], 2 * CH), BF16),
            jax.ShapeDtypeStruct(power.shape, F32),
        ),
        in_specs=[pl.BlockSpec(memory_space=pltpu.VMEM)] * 3,
        out_specs=(hbm, hbm),
        scratch_shapes=[pltpu.SemaphoreType.DMA((3,))],
        name="outputs",
    )(real, imag, power)


def solution(mesh):
    n_chan = mesh.shape["chan"]

    def body(vis, row_cell, tap_weight, tap_offset, block_tile, tile_owner, galaxy):
        nb = block_tile.shape[0]
        blocks = vis.reshape(nb, 2 * BR, vis.shape[2])
        cells = row_cell.reshape(nb, 1, BR)
        real, imag, power = fused(
            n_chan, (0, 1, 4, 11, 22, 33, 44), block_tile, tile_owner, tap_offset, cells, tap_weight, blocks, galaxy
        )
        return outputs(real, imag, power)

    return jax.shard_map(
        body,
        mesh=mesh,
        in_specs=(
            P("uv", None, "chan"),
            P("uv"),
            P(None, "uv"),
            P(),
            P("uv"),
            P(),
            P("uv", "chan", None),
        ),
        out_specs=(P("uv", "chan", None), P("uv", None)),
        check_vma=False,
    )
```

```python
import functools
import math

import jax
import jax.numpy as jnp
import numpy as np
from jax import lax
from jax.experimental import pallas as pl
from jax.experimental.pallas import tpu as pltpu
from jax.sharding import PartitionSpec as P

MESH = pl.DeviceIdType.MESH
CH = 1024
BR = 128
TC = 128
KT = 8
N_OWN = 16
CAP = 11
SLOTS = 19
BLOCKS = 96
TILES = 160
SIDE = 4
ORDER = (2, 1, 3, 0)
F32 = jnp.float32
BF16 = jnp.bfloat16
MIB = 2**20


def table_constant(n_chan):
    freq = np.arange(CH, dtype=np.int64)
    phase = ((freq[:, None] * freq[None, :]) % CH).astype(np.float32) * np.float32(2.0 * math.pi / CH)
    cosine, sine = np.cos(phase), np.sin(phase)
    x = freq.astype(np.float32) * np.float32(2.0 * math.pi / CH)
    taper = (
        np.float32(0.35875)
        - np.float32(0.48829) * np.cos(x)
        + np.float32(0.14128) * np.cos(np.float32(2.0) * x)
        - np.float32(0.01168) * np.cos(np.float32(3.0) * x)
    )
    scale = (taper / np.float32(math.sqrt(CH)))[:, None]
    upper = np.concatenate([cosine * scale, -sine * scale], axis=1)
    lower = np.concatenate([sine * scale, cosine * scale], axis=1)
    table = np.stack([upper, lower]).reshape(2, n_chan, CH // n_chan, 2 * CH)
    return table.transpose(1, 0, 2, 3).reshape(2 * CH, 2 * CH).astype(jnp.bfloat16)


def peer(uv, chan, dx=0, dy=0):
    x = lax.rem(uv // SIDE + dx, SIDE)
    y = lax.rem(lax.rem(uv, SIDE) + dy, SIDE)
    return (x * SIDE + y, chan)


def column(row):
    return jnp.transpose(jnp.broadcast_to(row, (128, 128)))


def tall(row):
    return jnp.concatenate([column(row[:, :128]), column(row[:, 128:])], axis=0)


def position_in_order(d):
    return jnp.where(d == 2, 0, jnp.where(d == 1, 1, jnp.where(d == 3, 2, 3)))


def count(mask):
    return jnp.where(mask, 1, 0)


def make_tables(x, y, tb, lists, places):
    tile_r, own_r = tb[0:1, :128], tb[1:2, :]
    lane = lax.broadcasted_iota(jnp.int32, (128, 128), 1)
    sub = lax.broadcasted_iota(jnp.int32, (128, 128), 0)
    tile_c = column(tile_r)
    lane_t = lax.broadcasted_iota(jnp.int32, (256, 128), 1)
    t_c = lax.broadcasted_iota(jnp.int32, (256, 128), 0)
    own_c = tall(own_r)
    match = tile_r == t_c
    number_c = jnp.sum(count(match), axis=1, keepdims=True)
    number_r = [jnp.sum(count(tile_c == lane + 128 * i), axis=0, keepdims=True) for i in range(2)]
    same = [own_r[:, 128 * i : 128 * (i + 1)] == own_c for i in range(2)]
    rank_c = sum(jnp.sum(count(same[i] & (lane_t + 128 * i < t_c)), axis=1, keepdims=True) for i in range(2))
    earlier_r = jnp.sum(count((tile_c == tile_r) & (sub < lane)), axis=0, keepdims=True)
    repeat_c = count(column(earlier_r) > 0)
    dx_c, dy_c = ((own_c >> 2) - x) & 3, ((own_c & 3) - y) & 3
    slot_key = jnp.where(t_c < TILES, own_c * 32 + rank_c, -1)
    start_c = sum(
        jnp.sum(jnp.where(same[i] & (lane_t + 128 * i < t_c), number_r[i], 0), axis=1, keepdims=True) for i in range(2)
    )
    last_c = jnp.where(number_c > 0, start_c + number_c, 0)
    for i in range(4):
        hit = slot_key == lane_t + 128 * i
        places[i : i + 1, :] = jnp.sum(jnp.where(hit, last_c, 0), axis=0, keepdims=True) - 1
    for h in range(2):
        group_c, inner_c = (dx_c, dy_c) if h == 0 else (dy_c, dx_c)
        first_c = group_c * 64 + position_in_order(inner_c) * CAP + start_c
        key_r = jnp.sum(jnp.where(match, first_c, 0), axis=0, keepdims=True) + earlier_r
        key_c = column(jnp.where(lane[0:1] < BLOCKS, key_r, -1))
        for i in range(2):
            hit = key_c == lane + 128 * i
            row = 4 * h + i
            lists[row : row + 1, :] = jnp.sum(jnp.where(hit, sub, 0), axis=0, keepdims=True)
            lists[row + 2 : row + 3, :] = jnp.sum(jnp.where(hit, repeat_c, 0), axis=0, keepdims=True)


def kernel(
    n_chan, cuts,
    block_tile, tile_owner, tap_offset, cells, tap_weight, vis_hbm, table_hbm, galaxy_hbm,
    real, imag, power,
    vis, wide, weight, table, galaxy, tb, lists, places, lists_sm, places_sm, carry, send, rec0, rec1, rec2, rec3, part, via, got, piece, flat,
    mine, mine_sent, others, last_sent, last_others,
    load_sem, msend, mrecv, sm_sem, asend, arecv, bsend, brecv, vsend, vrecv, zsend, zrecv, zlocal, psend, precv,
):
    uv, chan = lax.axis_index("uv"), lax.axis_index("chan")
    x, y = uv // SIDE, lax.rem(uv, SIDE)
    rows = TC // n_chan
    width = vis.shape[-1]
    recs = (rec0, rec1, rec2, rec3)

    def z_peer(d):
        return (uv, lax.rem(chan + d, n_chan))

    def xy_peer(h, d):
        return peer(uv, chan, dx=d) if h == 0 else peer(uv, chan, dy=d)

    loads = [
        pltpu.make_async_copy(table_hbm, table, load_sem.at[0]),
        pltpu.make_async_copy(galaxy_hbm, galaxy, load_sem.at[1]),
    ]
    quarter = BLOCKS // 4
    vis_loads = [
        pltpu.make_async_copy(
            vis_hbm.at[pl.ds(i * quarter, quarter)], vis.at[pl.ds(i * quarter, quarter)], load_sem.at[2 + i]
        )
        for i in range(4)
    ]
    for load in vis_loads:
        load.start()
    barrier = pltpu.get_barrier_semaphore()
    for h in range(2):
        for d in range(1, SIDE):
            pl.semaphore_signal(barrier, inc=1, device_id=xy_peer(h, d), device_id_type=MESH)
    for d in range(1, n_chan):
        pl.semaphore_signal(barrier, inc=1, device_id=z_peer(d), device_id_type=MESH)

    tb[...] = jnp.full(tb.shape, -1, jnp.int32)
    tb[0:1, 0 : block_tile.shape[1]] = block_tile[...]
    tb[1:2, 0 : tile_owner.shape[1]] = tile_owner[...]
    make_tables(x, y, tb, lists, places.at[0])
    places[SIDE] = places[0]
    to_scalars = pltpu.make_async_copy(lists, lists_sm, sm_sem.at[0])
    to_scalars.start()

    def split(i, _):
        for j in range(4):
            b = 4 * i + j
            weight[b] = tap_weight[:, pl.ds(pl.multiple_of(b * BR, BR), BR)].astype(F32)
            wide[2 * BR * j : 2 * BR * (j + 1), :] = vis[b].astype(F32)
            for part_of in range(2):
                rows_of = wide[pl.ds(2 * BR * j + part_of, BR, stride=2), :]
                vis[b, BR * part_of : BR * (part_of + 1), :] = rows_of.astype(BF16)
        return 0

    for i, load in enumerate(vis_loads):
        load.wait()
        lax.fori_loop(i * quarter // 4, (i + 1) * quarter // 4, split, 0)
    pl.semaphore_wait(barrier, 2 * (SIDE - 1) + n_chan - 1)

    def places_copy(h, d):
        k = h * SIDE + d
        return pltpu.make_async_remote_copy(
            places.at[0], places.at[k], msend.at[k], mrecv.at[k], device_id=xy_peer(h, d), device_id_type=MESH
        )

    for h in range(2):
        for d in range(1, SIDE):
            if h == 0:
                places_copy(h, d).start()
    for d in range(1, SIDE):
        places_copy(1, d).start()
    carry[...] = jnp.zeros_like(carry)
    mine_sent[...] = jnp.zeros_like(mine_sent)
    to_scalars.wait()
    loads[0].start()
    loads[1].start()

    def a_copy(h, g, k):
        n, size = cuts[k] // CAP, cuts[k + 1] - cuts[k]
        return pltpu.make_async_remote_copy(
            send.at[h, g - 1, pl.ds(cuts[k], size)], recs[n].at[h, g, pl.ds(cuts[k] - n * CAP, size)], asend.at[h, g - 1, k], arecv.at[h, g - 1, k],
            device_id=xy_peer(h, g), device_id_type=MESH,
        )

    cell_rows = lax.broadcasted_iota(jnp.int32, (TC, BR), 0)

    def place(n, p, _):
        for g in ORDER:
            for h in range(2):
                row, at = 4 * h + g // 2, 64 * (g % 2) + p
                b = jnp.minimum(lists_sm[row, at], BLOCKS - 1)
                keep = lists_sm[row + 2, at].astype(F32)
                away = cell_rows - cells[b]
                w = weight[b]
                matrix = jnp.zeros((TC, BR), F32)
                for k in range(KT):
                    matrix = matrix + jnp.where(away == tap_offset[k], w[k : k + 1, :], 0.0)
                half = vis[b, BR * h : BR * (h + 1), :]
                out = jnp.dot(matrix.astype(BF16), half, preferred_element_type=F32)
                out = out + keep * carry[h, g]
                carry[h, g] = out
                if g == 0:
                    recs[n][h, 0, p - n * CAP] = out.astype(BF16)
                else:
                    send[h, g - 1, p] = out.astype(BF16)
        return 0

    n_cuts = len(cuts) - 1
    for k in range(n_cuts):
        lax.fori_loop(cuts[k], cuts[k + 1], functools.partial(place, cuts[k] // CAP), 0)
        for g in ORDER[:3]:
            for h in range(2):
                a_copy(h, g, k).start()

    for h in range(2):
        for d in range(1, SIDE):
            places_copy(h, d).wait()
    places_load = pltpu.make_async_copy(places, places_sm, sm_sem.at[1])
    places_load.start()
    places_load.wait()

    slot_cuts = (0, 5, 10, 15, SLOTS)
    n_slot_cuts = len(slot_cuts) - 1
    middle = 10

    def b_copy(h, off, q):
        cut = pl.ds(slot_cuts[q], slot_cuts[q + 1] - slot_cuts[q])
        k = off // 2
        return pltpu.make_async_remote_copy(
            part.at[h, off - 1, cut], got.at[h, 1 + k, cut], bsend.at[h, k, q], brecv.at[h, k, q],
            device_id=xy_peer(1 - h, off), device_id_type=MESH,
        )

    def via_copy(h, k):
        cut = pl.ds(middle * k, middle if k == 0 else SLOTS - middle)
        return pltpu.make_async_remote_copy(
            part.at[h, 1, cut], via.at[h, cut], vsend.at[h, k], vrecv.at[h, k],
            device_id=xy_peer(1 - h, 1 if k == 0 else SIDE - 1), device_id_type=MESH,
        )

    arrived = 0
    for n, off in enumerate(ORDER):
        needed = CAP * (n + 1)
        while cuts[arrived] < needed:
            for h in range(2):
                for g in range(1, SIDE):
                    a_copy(h, g, arrived).wait_recv()
            arrived += 1
        for h in range(2):
            ox = x if h == 0 else lax.rem(x + off, SIDE)
            oy = lax.rem(y + off, SIDE) if h == 0 else y

            def one(add, s, _, h=h, off=off, rec=recs[n], ox=ox, oy=oy):
                total = via[h, s].astype(F32) if add else jnp.zeros((TC, width), F32)
                for d in range(SIDE):
                    p = places_sm[h * SIDE + d, ox, 32 * oy + s]
                    there = jnp.where(p >= 0, F32(1.0), F32(0.0))
                    at = jnp.clip(p, 0, CAP - 1)
                    total = total + there * rec[h, d, at].astype(F32)
                if off == 0:
                    got[h, 0, s] = total.astype(BF16)
                else:
                    part[h, off - 1, s] = total.astype(BF16)
                return 0

            if off in (0, 2):
                lax.fori_loop(0, SLOTS, functools.partial(one, False), 0)
                if off:
                    via_copy(h, 0).start()
                    via_copy(h, 1).start()
            else:
                via_copy(h, off // 2).wait_recv()
                for q in range(n_slot_cuts):
                    add = (slot_cuts[q] < middle) == (off == 1)
                    lax.fori_loop(slot_cuts[q], slot_cuts[q + 1], functools.partial(one, add), 0)
                    b_copy(h, off, q).start()

    def z_copy(d, q):
        there = lax.rem(chan + d, n_chan)
        columns = pl.ds(pl.multiple_of(chan * 2 * width, 2 * width), 2 * width)
        cut = pl.ds(slot_cuts[q], slot_cuts[q + 1] - slot_cuts[q])
        if d == 0:
            return pltpu.make_async_copy(piece.at[there, cut], flat.at[cut, :, columns], zlocal.at[q])
        return pltpu.make_async_remote_copy(
            piece.at[there, cut], flat.at[cut, :, columns], zsend.at[d - 1, q], zrecv.at[d - 1, q],
            device_id=z_peer(d), device_id_type=MESH,
        )

    def one_slot(s, _):
        for h in range(2):
            total = got[h, 0, s].astype(F32) + got[h, 1, s].astype(F32) + got[h, 2, s].astype(F32)
            piece[:, s, :, h * width : (h + 1) * width] = total.astype(BF16).reshape(n_chan, rows, width)
        return 0

    for q in range(n_slot_cuts):
        for h in range(2):
            for off in (1, 3):
                b_copy(h, off, q).wait_recv()
        lax.fori_loop(slot_cuts[q], slot_cuts[q + 1], one_slot, 0)
        for d in (*range(1, n_chan), 0):
            z_copy(d, q).start()
    loads[0].wait()
    loads[1].wait()

    step = 256
    def p_copy(d, i):
        return pltpu.make_async_remote_copy(
            (mine_sent, last_sent)[i], (others, last_others)[i].at[d - 1], psend.at[d - 1, i], precv.at[d - 1, i],
            device_id=z_peer(d), device_id_type=MESH,
        )

    parts = ((0, slot_cuts[-2]), (slot_cuts[-2], SLOTS))
    for i, (lo_s, hi_s) in enumerate(parts):
        for q in range(n_slot_cuts):
            if lo_s <= slot_cuts[q] < hi_s:
                z_copy(0, q).wait()
                for d in range(1, n_chan):
                    z_copy(d, q).wait_recv()
        v = flat[lo_s:hi_s].reshape((hi_s - lo_s) * rows, 2 * CH)
        for c in range(CH // step):
            lo = slice(c * step, (c + 1) * step)
            hi = slice(CH + c * step, CH + (c + 1) * step)
            re = jnp.dot(v, table[:, lo], preferred_element_type=F32).reshape(hi_s - lo_s, rows, step)
            im = jnp.dot(v, table[:, hi], preferred_element_type=F32).reshape(hi_s - lo_s, rows, step)
            real[lo_s:hi_s, :, lo] = re.astype(BF16)
            imag[lo_s:hi_s, :, lo] = im.astype(BF16)
            product = re * galaxy[lo_s:hi_s, :, lo].astype(F32) + im * galaxy[lo_s:hi_s, :, hi].astype(F32)
            sums = jnp.sum(product, axis=1)
            mine[lo_s:hi_s, lo] = sums
            if i == 0:
                mine_sent[0 : hi_s - lo_s, lo] = sums.astype(BF16)
            else:
                last_sent[4 * c : 4 * c + 4, :] = sums.astype(BF16)
        for d in range(1, n_chan):
            p_copy(d, i).start()

    for h in range(2):
        for g in range(1, SIDE):
            for k in range(n_cuts):
                a_copy(h, g, k).wait_send()
        for k in range(2):
            via_copy(h, k).wait_send()
            for q in range(n_slot_cuts):
                b_copy(h, 2 * k + 1, q).wait_send()
    for d in range(1, n_chan):
        for q in range(n_slot_cuts):
            z_copy(d, q).wait_send()
        for i in range(2):
            p_copy(d, i).wait_send()
    first = slot_cuts[-2]
    total = mine[:first, :]
    for d in range(1, n_chan):
        p_copy(d, 0).wait_recv()
        total = total + others[d - 1, :first, :].astype(F32)
    power[:first, :] = total / F32(math.sqrt(TC))
    for d in range(1, n_chan):
        p_copy(d, 1).wait_recv()
    for c in range(CH // step):
        columns = slice(c * step, (c + 1) * step)
        total = mine[first:, columns]
        for d in range(1, n_chan):
            total = total + last_others[d - 1, 4 * c : 4 * c + 4, :].astype(F32)
        power[first:, columns] = total / F32(math.sqrt(TC))


def fused(n_chan, cuts, block_tile, tile_owner, tap_offset, cells, weight, vis, galaxy):
    nb, _, width = vis.shape
    n_cuts = len(cuts) - 1
    rows = TC // n_chan
    smem = pl.BlockSpec(memory_space=pltpu.SMEM)
    vmem = pl.BlockSpec(memory_space=pltpu.VMEM)
    hbm = pl.BlockSpec(memory_space=pl.ANY)
    dma = pltpu.SemaphoreType.DMA
    return pl.pallas_call(
        functools.partial(kernel, n_chan, cuts),
        out_shape=(
            jax.ShapeDtypeStruct((SLOTS, rows, CH), BF16),
            jax.ShapeDtypeStruct((SLOTS, rows, CH), BF16),
            jax.ShapeDtypeStruct((SLOTS, CH), F32),
        ),
        in_specs=[vmem, vmem, smem, vmem, vmem, hbm, hbm, hbm],
        out_specs=(vmem, vmem, vmem),
        scratch_shapes=[
            pltpu.VMEM(vis.shape, BF16),
            pltpu.VMEM((4 * 2 * BR, width), F32),
            pltpu.VMEM((nb, KT, BR), F32),
            pltpu.VMEM((2 * CH, 2 * CH), BF16),
            pltpu.VMEM(galaxy.shape, BF16),
            pltpu.VMEM((8, 256), jnp.int32),
            pltpu.VMEM((8, 128), jnp.int32),
            pltpu.VMEM((2 * SIDE, 8, 128), jnp.int32),
            pltpu.SMEM((8, 128), jnp.int32),
            pltpu.SMEM((2 * SIDE, 8, 128), jnp.int32),
            pltpu.VMEM((2, SIDE, TC, width), F32),
            pltpu.VMEM((2, SIDE - 1, SIDE * CAP, TC, width), BF16),
            *[pltpu.VMEM((2, SIDE, CAP, TC, width), BF16) for _ in range(SIDE)],
            pltpu.VMEM((2, SIDE - 1, SLOTS, TC, width), BF16),
            pltpu.VMEM((2, SLOTS, TC, width), BF16),
            pltpu.VMEM((2, SIDE - 1, SLOTS, TC, width), BF16),
            pltpu.VMEM((n_chan, SLOTS, rows, 2 * width), BF16),
            pltpu.VMEM((SLOTS, rows, 2 * CH), BF16),
            pltpu.VMEM((SLOTS, CH), F32),
            pltpu.VMEM((16, CH), BF16),
            pltpu.VMEM((n_chan - 1, 16, CH), BF16),
            pltpu.VMEM((16, CH // 4), BF16),
            pltpu.VMEM((n_chan - 1, 16, CH // 4), BF16),
            dma((6,)),
            dma((2 * SIDE,)),
            dma((2 * SIDE,)),
            dma((2,)),
            dma((2, SIDE - 1, n_cuts)),
            dma((2, SIDE - 1, n_cuts)),
            dma((2, 2, 4)),
            dma((2, 2, 4)),
            dma((2, 2)),
            dma((2, 2)),
            dma((n_chan - 1, 4)),
            dma((n_chan - 1, 4)),
            dma((4,)),
            dma((n_chan - 1, 2)),
            dma((n_chan - 1, 2)),
        ],
        compiler_params=pltpu.CompilerParams(collective_id=0, has_side_effects=True, vmem_limit_bytes=60 * MIB),
        name="grid_delay",
    )(
        block_tile.reshape(1, -1), tile_owner.reshape(1, -1), tap_offset, cells, weight,
        vis, jnp.asarray(table_constant(n_chan)), galaxy,
    )


def outputs_kernel(real, imag, power, cube, power_out, held, held_power, sem):
    loads, stores = [], []
    cuts = (0, 5, 10, 15, SLOTS)
    for k, half in enumerate((real, imag)):
        for i in range(4):
            cut = pl.ds(cuts[i], cuts[i + 1] - cuts[i])
            n = len(loads)
            loads.append(pltpu.make_async_copy(half.at[cut], held.at[k, cut], sem.at[0, n]))
            stores.append(pltpu.make_async_copy(held.at[k, cut], cube.at[cut, :, pl.ds(k * CH, CH)], sem.at[1, n]))
    loads.append(pltpu.make_async_copy(power, held_power, sem.at[0, 8]))
    stores.append(pltpu.make_async_copy(held_power, power_out, sem.at[1, 8]))
    for load in loads:
        load.start()
    for load, store in zip(loads, stores):
        load.wait()
        store.start()
    for store in stores:
        store.wait()


def outputs(real, imag, power):
    hbm = pl.BlockSpec(memory_space=pl.ANY)
    return pl.pallas_call(
        outputs_kernel,
        out_shape=(
            jax.ShapeDtypeStruct((*real.shape[:2], 2 * CH), BF16),
            jax.ShapeDtypeStruct(power.shape, F32),
        ),
        in_specs=[hbm] * 3,
        out_specs=(hbm, hbm),
        scratch_shapes=[
            pltpu.VMEM((2, *real.shape), BF16),
            pltpu.VMEM(power.shape, F32),
            pltpu.SemaphoreType.DMA((2, 9)),
        ],
        name="outputs",
    )(real, imag, power)


def solution(mesh):
    n_chan = mesh.shape["chan"]

    def body(vis, row_cell, tap_weight, tap_offset, block_tile, tile_owner, galaxy):
        nb = block_tile.shape[0]
        blocks = vis.reshape(nb, 2 * BR, vis.shape[2])
        cells = row_cell.reshape(nb, 1, BR)
        real, imag, power = fused(
            n_chan, (0, 1, 4, 11, 22, 33, 44), block_tile, tile_owner, tap_offset, cells, tap_weight, blocks, galaxy
        )
        return outputs(real, imag, power)

    return jax.shard_map(
        body,
        mesh=mesh,
        in_specs=(
            P("uv", None, "chan"),
            P("uv"),
            P(None, "uv"),
            P(),
            P("uv"),
            P(),
            P("uv", "chan", None),
        ),
        out_specs=(P("uv", "chan", None), P("uv", None)),
        check_vma=False,
    )
```
